32 devices in a mesh: fsdp: 4 (over z), grp: 8 (over y, x, core).
Axes of the slice: x: 2, y: 2, z: 4, core: 2. Of those that a mesh axis runs over, the one named last changes fastest.
Arguments:
- grads: bfloat16 [16, 384, 2048], P('grp', 'fsdp')
- momentum: bfloat16 [16, 384, 2048], P('grp', 'fsdp'), may hold values from -6 to 6
- row_counts: int32 [16], P('grp'), may hold values from 128 to 384, as said below
Outputs:
- update: bfloat16 [16, 384, 2048], P('grp', 'fsdp')
- new_momentum: bfloat16 [16, 384, 2048], P('grp', 'fsdp')
The draws below stay inside these ranges and needn't reach their ends.
Inputs may be any that keep to these rules, and one draw needn't show every extreme that they name: `row_counts`: each entry is one, two or three times 384 // 3, and some entry equals 384.
All inputs are finite; a program needn't handle non-finite values.
Results may differ from the reference program's by a relative error of at most 0.007.
Values may be sent and summed in bfloat16 or wider, within the bound.
A program may use at most 64 MiB of HBM per device.

```python
import math
import jax
import jax.numpy as jnp
from jax import lax

D = 2048
ROWS = 384
ITERS = 2
NMAT = 16


def draw_grads(key, part):
    first, second = jax.random.split(jax.random.fold_in(key, 11))
    matrix_ids = jnp.arange(NMAT, dtype=jnp.float32)[:, None, None]
    row_frac = jnp.arange(ROWS, dtype=jnp.float32)[None, :, None] / ROWS
    position = matrix_ids / NMAT
    rough = jax.random.uniform(first, (NMAT, ROWS, 1), minval=0.0, maxval=math.log(2.0))
    base = jax.random.normal(second, (NMAT, ROWS, D))
    scale = (1.0 + 4.0 * row_frac) * (1.0 + 0.5 * position) * jnp.exp(rough)
    return (base * scale).astype(jnp.bfloat16)


def draw_row_counts(key, part):
    level = jax.random.randint(jax.random.fold_in(key, 5), (NMAT,), 1, 5)
    level = jnp.minimum(level, 3)
    level = jnp.where(jnp.arange(NMAT) == 0, 3, level)
    return (level * (ROWS // 3)).astype(jnp.int32)


def block_levels(rng, extent, cuts, smallest, largest):
    level, own = 1.0, jax.random.fold_in(rng, 6)
    for dim, blocks in cuts:
        steps = jnp.exp(jax.random.uniform(jax.random.fold_in(own, dim), (blocks,), jnp.float32, smallest / len(cuts), largest / len(cuts)))
        level = level * jnp.repeat(steps, extent[dim] // blocks).reshape([-1 if axis == dim else 1 for axis in range(len(extent))])
    return level


def bell_draw(rng, dims, spread, limit, pieces=(), kind=jnp.bfloat16):
    drawn = spread * jax.random.normal(rng, dims, jnp.float32)
    if pieces:
        drawn = drawn * block_levels(rng, dims, pieces, -0.22, 0.18)
    return jnp.clip(drawn, -limit, limit).astype(kind)


def setup_inputs(seed: int = 0) -> dict:
    splits = jax.random.split(jax.random.key(seed), 4)
    return {
        "grads": draw_grads(jax.random.fold_in(splits[3], 71), 0),
        "momentum": bell_draw(splits[1], (NMAT, ROWS, D), 1.0, 6.0, ((0, 8), (1, 4))),
        "row_counts": draw_row_counts(jax.random.fold_in(splits[3], 71), 0),
    }


first_coef = 3.4445
second_coef = -4.775
third_coef = 2.0315

def orthogonal(matrix):
    frob = jnp.sqrt(jnp.sum(jnp.square(matrix.astype(jnp.float32))))
    current = (matrix.astype(jnp.float32) / (frob + 1e-07)).astype(jnp.bfloat16)
    for step in range(ITERS):
        gram = jnp.dot(current, current.T, preferred_element_type=jnp.float32).astype(jnp.bfloat16)
        square = jnp.dot(gram, gram, preferred_element_type=jnp.float32)
        poly = (second_coef * gram.astype(jnp.float32) + third_coef * square).astype(jnp.bfloat16)
        current = (first_coef * current.astype(jnp.float32) + jnp.dot(poly, current, preferred_element_type=jnp.float32)).astype(jnp.bfloat16)
    return current

def reference(grads, momentum, row_counts):
    row_ids = jnp.arange(ROWS, dtype=jnp.int32)
    live = row_ids[None, :, None] < row_counts[:, None, None]
    graded = jnp.where(live, grads.astype(jnp.float32), 0.0)
    total_rows = jnp.sum(row_counts).astype(jnp.float32)
    square_mean = jnp.sum(graded * graded) / (total_rows * D)
    clip = jnp.minimum(1.0, lax.rsqrt(square_mean + 1e-06))
    new_momentum = jnp.where(live, 0.95 * momentum.astype(jnp.float32) + clip * graded, 0.0).astype(jnp.bfloat16)
    result = lax.map(orthogonal, new_momentum)
    update = (0.2 * jnp.sqrt(jnp.float32(D)) * result.astype(jnp.float32)).astype(jnp.bfloat16)
    return (update, new_momentum)
```

```python
import functools
import math

import jax
import jax.numpy as jnp
from jax import lax
from jax.experimental import pallas as pl
from jax.experimental.pallas import tpu as pltpu
from jax.sharding import PartitionSpec as P

ITERS = 2

first_coef = 3.4445
second_coef = -4.775
third_coef = 2.0315

ROW_STEP = 16
SEND_COLS = 512


def kernel(
    groups, size, paired,
    counts_ref, grads_hbm, momentum_hbm, update_hbm, new_hbm,
    grads, momentum, fresh, owned, gram_out, gram_in, result, fsdp_sums, grp_sums,
    load_sem, store_sem, own_sem,
    fsdp_send, fsdp_recv, grp_send, grp_recv,
    out_send, out_recv, gram_send, gram_recv, back_send, back_recv,
):
    matrices, rows, width = grads.shape
    half = width // 2
    step_cols = math.gcd(half, SEND_COLS)
    steps = half // step_cols
    f = lax.axis_index("fsdp")
    g = lax.axis_index("grp")

    def dev(a, b):
        return {"fsdp": a, "grp": b}

    if paired:
        core = lax.rem(g, 2)
        base = g - core
        owner_g = base + f // matrices
        owner_m = lax.rem(f, matrices)
        my_half = core
        peer = (f, base + 1 - core)

        def target(m, h):
            return core * matrices + m, base + h
    else:
        owner_g = g
        owner_m = f // 2
        my_half = lax.rem(f, 2)
        peer = (f + 1 - 2 * my_half, g)

        def target(m, h):
            return jnp.int32(2 * m + h), g

    barrier = pltpu.get_barrier_semaphore()
    others = [(lax.rem(f + d, size), g) for d in range(1, size)]
    others += [(f, lax.rem(g + d, groups)) for d in range(1, groups)]
    if paired:
        others += [(lax.rem(f + d, size), base + 1 - core) for d in range(1, size)]
    for a, b in others:
        pl.semaphore_signal(barrier, inc=1, device_id=dev(a, b), device_id_type=pl.DeviceIdType.MESH)

    load_grads = pltpu.make_async_copy(grads_hbm, grads, load_sem.at[0])
    load_momentum = pltpu.make_async_copy(momentum_hbm, momentum, load_sem.at[1])
    load_grads.start()
    load_momentum.start()

    offset = f * rows

    def live_mask(m, r):
        ids = offset + r + lax.broadcasted_iota(jnp.int32, (ROW_STEP, 1), 0)
        return ids < counts_ref[m]

    load_grads.wait()
    acc = jnp.zeros((8, width), jnp.float32)
    for m in range(matrices):
        for r in range(0, rows, ROW_STEP):
            part = jnp.where(live_mask(m, r), grads[m, r:r + ROW_STEP, :].astype(jnp.float32), 0.0)
            part = part * part
            for k in range(0, ROW_STEP, 8):
                acc = acc + part[k:k + 8]
    tile = acc[:, :128]
    for k in range(128, width, 128):
        tile = tile + acc[:, k:k + 128]
    live_rows = jnp.int32(0)
    for m in range(matrices):
        live_rows = live_rows + jnp.clip(counts_ref[m] - offset, 0, rows)
    fsdp_sums[f, 0:8, :] = tile
    fsdp_sums[f, 8:16, :] = jnp.zeros((8, 128), jnp.float32) + live_rows.astype(jnp.float32)

    pl.semaphore_wait(barrier, len(others))

    def exchange(buf, me, count, place, send, recv):
        copies = []
        for d in range(1, count):
            a, b = place(lax.rem(me + d, count))
            copy = pltpu.make_async_remote_copy(
                buf.at[me], buf.at[me], send.at[d], recv.at[d],
                device_id=dev(a, b), device_id_type=pl.DeviceIdType.MESH,
            )
            copy.start()
            copies.append(copy)
        for copy in copies:
            copy.wait_recv()
        total = buf[0]
        for d in range(1, count):
            total = total + buf[d]
        return total, copies

    total, fsdp_copies = exchange(fsdp_sums, f, size, lambda i: (i, g), fsdp_send, fsdp_recv)
    grp_sums[g] = total
    load_momentum.wait()
    total, grp_copies = exchange(grp_sums, g, groups, lambda i: (f, i), grp_send, grp_recv)
    square_sum = jnp.sum(total[0:8], keepdims=True)
    row_total = total[8:9, 0:1]
    clip = jnp.minimum(1.0, lax.rsqrt(square_sum / (row_total * width) + 1e-06))

    def out_copy(m, h):
        a, b = target(m, h)
        copy = pltpu.make_async_remote_copy(
            fresh.at[m, :, pl.ds(h * half, half)],
            owned.at[pl.ds(pl.multiple_of(f * rows, 16), rows), :],
            out_send.at[m * 2 + h], out_recv.at[f],
            device_id=dev(a, b), device_id_type=pl.DeviceIdType.MESH,
        )
        return copy, jnp.logical_and(a == f, b == g)

    for m in range(matrices):
        for h in range(2):
            cols = slice(h * half, (h + 1) * half)
            for r in range(0, rows, ROW_STEP):
                at = (m, slice(r, r + ROW_STEP), cols)
                fresh[at] = jnp.where(
                    live_mask(m, r),
                    0.95 * momentum[at].astype(jnp.float32) + clip * grads[at].astype(jnp.float32),
                    0.0,
                ).astype(jnp.bfloat16)
            copy, mine = out_copy(m, h)

            @pl.when(jnp.logical_not(mine))
            def _():
                copy.start()

            @pl.when(mine)
            def _():
                owned[pl.ds(pl.multiple_of(f * rows, 16), rows), :] = fresh[m, :, cols]

    store_new = pltpu.make_async_copy(fresh, new_hbm, store_sem)
    store_new.start()

    def here(i):
        return jnp.logical_and(i == f, owner_g == g)

    for i in range(size):
        arrive = pltpu.make_async_remote_copy(
            fresh.at[0, :, pl.ds(0, half)], owned.at[pl.ds(i * rows, rows), :],
            out_send.at[0], out_recv.at[i],
            device_id=dev(f, owner_g), device_id_type=pl.DeviceIdType.MESH,
        )

        @pl.when(jnp.logical_not(here(i)))
        def _():
            arrive.wait_recv()

    def dot(a, b):
        return jnp.dot(a.astype(jnp.bfloat16), b.astype(jnp.bfloat16), preferred_element_type=jnp.float32)

    full = owned[...]
    gram = lax.dot_general(full, full, (((1,), (1,)), ((), ())), preferred_element_type=jnp.float32)
    gram_out[...] = gram.astype(jnp.bfloat16)
    gram_copy = pltpu.make_async_remote_copy(
        gram_out, gram_in, gram_send, gram_recv,
        device_id=dev(*peer), device_id_type=pl.DeviceIdType.MESH,
    )
    gram_copy.start()
    gram_copy.wait_recv()
    gram = gram + gram_in[...].astype(jnp.float32)
    order = gram.shape[0]
    diagonal = lax.broadcasted_iota(jnp.int32, (order, order), 0) == lax.broadcasted_iota(
        jnp.int32, (order, order), 1
    )
    trace = jnp.sum(jnp.where(diagonal, gram, 0.0), keepdims=True)
    inverse = 1.0 / (jnp.sqrt(trace) + 1e-07)
    gram = (gram * inverse) * inverse
    poly = second_coef * gram + third_coef * dot(gram, gram)
    mix = poly
    for _ in range(ITERS - 1):
        turned = dot(poly, gram)
        gram = first_coef * first_coef * gram + 2 * first_coef * turned + dot(poly, turned)
        before = poly
        poly = second_coef * gram + third_coef * dot(gram, gram)
        mix = first_coef * (before + poly) + dot(poly, before)
    lead = first_coef ** ITERS
    mix = mix.astype(jnp.bfloat16)
    scale = inverse * (0.2 * math.sqrt(width))

    def back_copy(i, j):
        copy = pltpu.make_async_remote_copy(
            result.at[j, pl.ds(i * rows, rows), :],
            update_hbm.at[
                owner_m, :, pl.ds(pl.multiple_of(my_half * half + j * step_cols, step_cols), step_cols)
            ],
            back_send.at[i * steps + j],
            back_recv.at[(owner_m * 2 + my_half) * steps + j],
            device_id=dev(jnp.int32(i), owner_g), device_id_type=pl.DeviceIdType.MESH,
        )
        local = pltpu.make_async_copy(
            result.at[j, pl.ds(i * rows, rows), :],
            update_hbm.at[
                owner_m, :, pl.ds(pl.multiple_of(my_half * half + j * step_cols, step_cols), step_cols)
            ],
            own_sem.at[j],
        )
        return copy, local

    for j in range(steps):
        block = owned[:, j * step_cols:(j + 1) * step_cols]
        made = lead * block.astype(jnp.float32) + jnp.dot(mix, block, preferred_element_type=jnp.float32)
        result[j] = (scale * made).astype(jnp.bfloat16)
        for i in range(size):
            copy, local = back_copy(i, j)

            @pl.when(jnp.logical_not(here(i)))
            def _():
                copy.start()

            @pl.when(here(i))
            def _():
                local.start()

    for copy in fsdp_copies + grp_copies:
        copy.wait_send()
    gram_copy.wait_send()
    for m in range(matrices):
        for h in range(2):
            copy, mine = out_copy(m, h)

            @pl.when(jnp.logical_not(mine))
            def _():
                copy.wait_send()

    store_new.wait()
    for j in range(steps):
        for i in range(size):
            copy, local = back_copy(i, j)

            @pl.when(jnp.logical_not(here(i)))
            def _():
                copy.wait_send()

            @pl.when(here(i))
            def _():
                local.wait()

    for m in range(matrices):
        for h in range(2):
            a, b = target(m, h)
            for j in range(steps):
                arrive = pltpu.make_async_remote_copy(
                    result.at[j, pl.ds(0, rows), :],
                    update_hbm.at[m, :, pl.ds(h * half + j * step_cols, step_cols)],
                    back_send.at[0], back_recv.at[(m * 2 + h) * steps + j],
                    device_id=dev(a, b), device_id_type=pl.DeviceIdType.MESH,
                )

                @pl.when(jnp.logical_not(jnp.logical_and(a == f, b == g)))
                def _():
                    arrive.wait_recv()


def local(groups, size, paired, grads, momentum, row_counts):
    matrices, rows, width = grads.shape
    half = width // 2
    step_cols = math.gcd(half, SEND_COLS)
    steps = half // step_cols
    order = size * rows
    dma = pltpu.SemaphoreType.DMA
    update, new_momentum = pl.pallas_call(
        functools.partial(kernel, groups, size, paired),
        out_shape=(
            jax.ShapeDtypeStruct(grads.shape, jnp.bfloat16),
            jax.ShapeDtypeStruct(grads.shape, jnp.bfloat16),
        ),
        in_specs=[
            pl.BlockSpec(memory_space=pltpu.SMEM),
            pl.BlockSpec(memory_space=pl.ANY),
            pl.BlockSpec(memory_space=pl.ANY),
        ],
        out_specs=(pl.BlockSpec(memory_space=pl.ANY), pl.BlockSpec(memory_space=pl.ANY)),
        scratch_shapes=[
            pltpu.VMEM(grads.shape, jnp.bfloat16),
            pltpu.VMEM(grads.shape, jnp.bfloat16),
            pltpu.VMEM(grads.shape, jnp.bfloat16),
            pltpu.VMEM((order, half), jnp.bfloat16),
            pltpu.VMEM((order, order), jnp.bfloat16),
            pltpu.VMEM((order, order), jnp.bfloat16),
            pltpu.VMEM((steps, order, step_cols), jnp.bfloat16),
            pltpu.VMEM((size, 16, 128), jnp.float32),
            pltpu.VMEM((groups, 16, 128), jnp.float32),
            dma((2,)),
            dma,
            dma((steps,)),
            dma((size,)),
            dma((size,)),
            dma((groups,)),
            dma((groups,)),
            dma((2 * matrices,)),
            dma((size,)),
            dma,
            dma,
            dma((size * steps,)),
            dma((2 * matrices * steps,)),
        ],
        compiler_params=pltpu.CompilerParams(
            collective_id=0, has_side_effects=True, vmem_limit_bytes=32 * 1024 * 1024
        ),
        cost_estimate=pl.CostEstimate(
            flops=4 * order * order * half, bytes_accessed=8 * grads.size, transcendentals=0
        ),
    )(row_counts, grads, momentum)
    return update, new_momentum


def chips_pair_groups(mesh):
    names = list(mesh.axis_names)
    grid = mesh.devices
    if names != ["fsdp", "grp"] or grid.shape[1] % 2:
        return False
    return all(
        getattr(grid[0, i], "coords", None) is not None
        and tuple(grid[0, i].coords) == tuple(grid[0, i + 1].coords)
        for i in range(0, grid.shape[1], 2)
    )


def solution(mesh):
    placed = (P("grp", "fsdp", None), P("grp", "fsdp", None), P("grp"))
    return jax.shard_map(
        functools.partial(local, mesh.shape["grp"], mesh.shape["fsdp"], chips_pair_groups(mesh)),
        mesh=mesh,
        in_specs=placed,
        out_specs=(P("grp", "fsdp", None), P("grp", "fsdp", None)),
        check_vma=False,
    )
```

```python
import functools
import math

import jax
import jax.numpy as jnp
from jax import lax
from jax.experimental import pallas as pl
from jax.experimental.pallas import tpu as pltpu
from jax.sharding import PartitionSpec as P

ITERS = 2

first_coef = 3.4445
second_coef = -4.775
third_coef = 2.0315

ROW_STEP = 16
SEND_COLS = 512
VMEM_BYTES = 63 * 1024 * 1024


def kernel(
    groups, size, paired,
    counts_hbm, grads_hbm, momentum_hbm, update_hbm, new_hbm,
    counts_ref, grads, momentum, fresh, owned, gram_out, gram_in, result, fsdp_sums, grp_sums,
    count_sem, load_sem, store_sem, own_sem,
    fsdp_send, fsdp_recv, grp_send, grp_recv,
    out_send, out_recv, gram_send, gram_recv, back_send, back_recv,
):
    matrices, rows, width = grads.shape
    half = width // 2
    step_cols = math.gcd(half, SEND_COLS)
    steps = half // step_cols
    f = lax.axis_index("fsdp")
    g = lax.axis_index("grp")

    def dev(a, b):
        return {"fsdp": a, "grp": b}

    if paired:
        core = lax.rem(g, 2)
        base = g - core
        owner_g = base + f // matrices
        owner_m = lax.rem(f, matrices)
        my_half = core
        peer = (f, base + 1 - core)

        def target(m, h):
            return core * matrices + m, base + h
    else:
        owner_g = g
        owner_m = f // 2
        my_half = lax.rem(f, 2)
        peer = (f + 1 - 2 * my_half, g)

        def target(m, h):
            return jnp.int32(2 * m + h), g

    barrier = pltpu.get_barrier_semaphore()
    others = [(lax.rem(f + d, size), g) for d in range(1, size)]
    others += [(f, lax.rem(g + d, groups)) for d in range(1, groups)]
    if paired:
        others += [(lax.rem(f + d, size), base + 1 - core) for d in range(1, size)]
    for a, b in others:
        pl.semaphore_signal(barrier, inc=1, device_id=dev(a, b), device_id_type=pl.DeviceIdType.MESH)

    load_counts = pltpu.make_async_copy(counts_hbm, counts_ref, count_sem)
    load_counts.start()
    piece = load_rows(rows)
    loads = [
        [
            pltpu.make_async_copy(
                source.at[m, pl.ds(r, piece), :], kept.at[m, pl.ds(r, piece), :],
                load_sem.at[k, m * (rows // piece) + r // piece],
            )
            for m in range(matrices)
            for r in range(0, rows, piece)
        ]
        for k, (source, kept) in enumerate(((grads_hbm, grads), (momentum_hbm, momentum)))
    ]
    for load in loads[0] + loads[1]:
        load.start()

    offset = f * rows

    def live_mask(m, r):
        ids = offset + r + lax.broadcasted_iota(jnp.int32, (ROW_STEP, 1), 0)
        return ids < counts_ref[m]

    load_counts.wait()
    acc = jnp.zeros((8, width), jnp.float32)
    for m in range(matrices):
        for r in range(0, rows, ROW_STEP):
            if r % piece == 0:
                loads[0][m * (rows // piece) + r // piece].wait()
            part = jnp.where(live_mask(m, r), grads[m, r:r + ROW_STEP, :].astype(jnp.float32), 0.0)
            part = part * part
            for k in range(0, ROW_STEP, 8):
                acc = acc + part[k:k + 8]
    tile = acc[:, :128]
    for k in range(128, width, 128):
        tile = tile + acc[:, k:k + 128]
    live_rows = jnp.int32(0)
    for m in range(matrices):
        live_rows = live_rows + jnp.clip(counts_ref[m] - offset, 0, rows)
    fsdp_sums[f, 0:8, :] = tile
    fsdp_sums[f, 8:16, :] = jnp.zeros((8, 128), jnp.float32) + live_rows.astype(jnp.float32)

    pl.semaphore_wait(barrier, len(others))

    def exchange(buf, me, count, place, send, recv):
        copies = []
        for d in range(1, count):
            a, b = place(lax.rem(me + d, count))
            copy = pltpu.make_async_remote_copy(
                buf.at[me], buf.at[me], send.at[d], recv.at[d],
                device_id=dev(a, b), device_id_type=pl.DeviceIdType.MESH,
            )
            copy.start()
            copies.append(copy)
        for copy in copies:
            copy.wait_recv()
        total = buf[0]
        for d in range(1, count):
            total = total + buf[d]
        return total, copies

    total, fsdp_copies = exchange(fsdp_sums, f, size, lambda i: (i, g), fsdp_send, fsdp_recv)
    grp_sums[g] = total
    for load in loads[1]:
        load.wait()
    total, grp_copies = exchange(grp_sums, g, groups, lambda i: (f, i), grp_send, grp_recv)
    square_sum = jnp.sum(total[0:8], keepdims=True)
    row_total = total[8:9, 0:1]
    clip = jnp.minimum(1.0, lax.rsqrt(square_sum / (row_total * width) + 1e-06))

    def out_copy(m, h):
        a, b = target(m, h)
        copy = pltpu.make_async_remote_copy(
            fresh.at[m, :, pl.ds(h * half, half)],
            owned.at[pl.ds(pl.multiple_of(f * rows, 16), rows), :],
            out_send.at[m * 2 + h], out_recv.at[f],
            device_id=dev(a, b), device_id_type=pl.DeviceIdType.MESH,
        )
        return copy, jnp.logical_and(a == f, b == g)

    for m in range(matrices):
        for h in range(2):
            cols = slice(h * half, (h + 1) * half)
            for r in range(0, rows, ROW_STEP):
                at = (m, slice(r, r + ROW_STEP), cols)
                fresh[at] = jnp.where(
                    live_mask(m, r),
                    0.95 * momentum[at].astype(jnp.float32) + clip * grads[at].astype(jnp.float32),
                    0.0,
                ).astype(jnp.bfloat16)
            copy, mine = out_copy(m, h)

            @pl.when(jnp.logical_not(mine))
            def _():
                copy.start()

            @pl.when(mine)
            def _():
                owned[pl.ds(pl.multiple_of(f * rows, 16), rows), :] = fresh[m, :, cols]

    store_new = pltpu.make_async_copy(fresh, new_hbm, store_sem)
    store_new.start()

    def here(i):
        return jnp.logical_and(i == f, owner_g == g)

    for i in range(size):
        arrive = pltpu.make_async_remote_copy(
            fresh.at[0, :, pl.ds(0, half)], owned.at[pl.ds(i * rows, rows), :],
            out_send.at[0], out_recv.at[i],
            device_id=dev(f, owner_g), device_id_type=pl.DeviceIdType.MESH,
        )

        @pl.when(jnp.logical_not(here(i)))
        def _():
            arrive.wait_recv()

    def dot(a, b):
        return jnp.dot(a.astype(jnp.bfloat16), b.astype(jnp.bfloat16), preferred_element_type=jnp.float32)

    full = owned[...]
    gram = lax.dot_general(full, full, (((1,), (1,)), ((), ())), preferred_element_type=jnp.float32)
    gram_out[...] = gram.astype(jnp.bfloat16)
    gram_copy = pltpu.make_async_remote_copy(
        gram_out, gram_in, gram_send, gram_recv,
        device_id=dev(*peer), device_id_type=pl.DeviceIdType.MESH,
    )
    gram_copy.start()
    gram_copy.wait_recv()
    gram = gram + gram_in[...].astype(jnp.float32)
    order = gram.shape[0]
    diagonal = lax.broadcasted_iota(jnp.int32, (order, order), 0) == lax.broadcasted_iota(
        jnp.int32, (order, order), 1
    )
    trace = jnp.sum(jnp.where(diagonal, gram, 0.0), keepdims=True)
    inverse = 1.0 / (jnp.sqrt(trace) + 1e-07)
    gram = (gram * inverse) * inverse
    poly = second_coef * gram + third_coef * dot(gram, gram)
    mix = poly
    for _ in range(ITERS - 1):
        turned = dot(poly, gram)
        gram = first_coef * first_coef * gram + 2 * first_coef * turned + dot(poly, turned)
        before = poly
        poly = second_coef * gram + third_coef * dot(gram, gram)
        mix = first_coef * (before + poly) + dot(poly, before)
    lead = first_coef ** ITERS
    mix = mix.astype(jnp.bfloat16)
    scale = inverse * (0.2 * math.sqrt(width))

    def back_copy(i, j):
        copy = pltpu.make_async_remote_copy(
            result.at[j, pl.ds(i * rows, rows), :],
            update_hbm.at[
                owner_m, :, pl.ds(pl.multiple_of(my_half * half + j * step_cols, step_cols), step_cols)
            ],
            back_send.at[i * steps + j],
            back_recv.at[(owner_m * 2 + my_half) * steps + j],
            device_id=dev(jnp.int32(i), owner_g), device_id_type=pl.DeviceIdType.MESH,
        )
        local = pltpu.make_async_copy(
            result.at[j, pl.ds(i * rows, rows), :],
            update_hbm.at[
                owner_m, :, pl.ds(pl.multiple_of(my_half * half + j * step_cols, step_cols), step_cols)
            ],
            own_sem.at[j],
        )
        return copy, local

    for j in range(steps):
        block = owned[:, j * step_cols:(j + 1) * step_cols]
        made = lead * block.astype(jnp.float32) + jnp.dot(mix, block, preferred_element_type=jnp.float32)
        result[j] = (scale * made).astype(jnp.bfloat16)
        for i in range(size):
            copy, local = back_copy(i, j)

            @pl.when(jnp.logical_not(here(i)))
            def _():
                copy.start()

            @pl.when(here(i))
            def _():
                local.start()

    for copy in fsdp_copies + grp_copies:
        copy.wait_send()
    gram_copy.wait_send()
    for m in range(matrices):
        for h in range(2):
            copy, mine = out_copy(m, h)

            @pl.when(jnp.logical_not(mine))
            def _():
                copy.wait_send()

    store_new.wait()
    for j in range(steps):
        for i in range(size):
            copy, local = back_copy(i, j)

            @pl.when(jnp.logical_not(here(i)))
            def _():
                copy.wait_send()

            @pl.when(here(i))
            def _():
                local.wait()

    for m in range(matrices):
        for h in range(2):
            a, b = target(m, h)
            for j in range(steps):
                arrive = pltpu.make_async_remote_copy(
                    result.at[j, pl.ds(0, rows), :],
                    update_hbm.at[m, :, pl.ds(h * half + j * step_cols, step_cols)],
                    back_send.at[0], back_recv.at[(m * 2 + h) * steps + j],
                    device_id=dev(a, b), device_id_type=pl.DeviceIdType.MESH,
                )

                @pl.when(jnp.logical_not(jnp.logical_and(a == f, b == g)))
                def _():
                    arrive.wait_recv()


def load_rows(rows):
    return 32 if rows % 32 == 0 else rows


def store(update, new, update_hbm, new_hbm, sems):
    copies = [
        pltpu.make_async_copy(source.at[m], kept.at[m], sems.at[k, m])
        for k, (source, kept) in enumerate(((update, update_hbm), (new, new_hbm)))
        for m in range(update.shape[0])
    ]
    for copy in copies:
        copy.start()
    for copy in copies:
        copy.wait()


def local(groups, size, paired, grads, momentum, row_counts):
    matrices, rows, width = grads.shape
    half = width // 2
    step_cols = math.gcd(half, SEND_COLS)
    steps = half // step_cols
    order = size * rows
    dma = pltpu.SemaphoreType.DMA
    update, new_momentum = pl.pallas_call(
        functools.partial(kernel, groups, size, paired),
        out_shape=(
            jax.ShapeDtypeStruct(grads.shape, jnp.bfloat16),
            jax.ShapeDtypeStruct(grads.shape, jnp.bfloat16),
        ),
        in_specs=[
            pl.BlockSpec(memory_space=pltpu.HBM),
            pl.BlockSpec(memory_space=pltpu.HBM),
            pl.BlockSpec(memory_space=pltpu.HBM),
        ],
        out_specs=(pl.BlockSpec(memory_space=pl.ANY), pl.BlockSpec(memory_space=pl.ANY)),
        scratch_shapes=[
            pltpu.SMEM(row_counts.shape, jnp.int32),
            pltpu.VMEM(grads.shape, jnp.bfloat16),
            pltpu.VMEM(grads.shape, jnp.bfloat16),
            pltpu.VMEM(grads.shape, jnp.bfloat16),
            pltpu.VMEM((order, half), jnp.bfloat16),
            pltpu.VMEM((order, order), jnp.bfloat16),
            pltpu.VMEM((order, order), jnp.bfloat16),
            pltpu.VMEM((steps, order, step_cols), jnp.bfloat16),
            pltpu.VMEM((size, 16, 128), jnp.float32),
            pltpu.VMEM((groups, 16, 128), jnp.float32),
            dma,
            dma((2, matrices * (rows // load_rows(rows)))),
            dma,
            dma((steps,)),
            dma((size,)),
            dma((size,)),
            dma((groups,)),
            dma((groups,)),
            dma((2 * matrices,)),
            dma((size,)),
            dma,
            dma,
            dma((size * steps,)),
            dma((2 * matrices * steps,)),
        ],
        compiler_params=pltpu.CompilerParams(
            collective_id=0, has_side_effects=True, vmem_limit_bytes=VMEM_BYTES
        ),
        cost_estimate=pl.CostEstimate(
            flops=4 * order * order * half, bytes_accessed=8 * grads.size, transcendentals=0
        ),
    )(row_counts, grads, momentum)
    return pl.pallas_call(
        store,
        out_shape=(
            jax.ShapeDtypeStruct(grads.shape, jnp.bfloat16),
            jax.ShapeDtypeStruct(grads.shape, jnp.bfloat16),
        ),
        in_specs=[pl.BlockSpec(memory_space=pl.ANY)] * 2,
        out_specs=(pl.BlockSpec(memory_space=pltpu.HBM), pl.BlockSpec(memory_space=pltpu.HBM)),
        scratch_shapes=[dma((2, matrices))],
        compiler_params=pltpu.CompilerParams(vmem_limit_bytes=VMEM_BYTES),
    )(update, new_momentum)


def chips_pair_groups(mesh):
    names = list(mesh.axis_names)
    grid = mesh.devices
    if names != ["fsdp", "grp"] or grid.shape[1] % 2:
        return False
    return all(
        getattr(grid[0, i], "coords", None) is not None
        and tuple(grid[0, i].coords) == tuple(grid[0, i + 1].coords)
        for i in range(0, grid.shape[1], 2)
    )


def solution(mesh):
    placed = (P("grp", "fsdp", None), P("grp", "fsdp", None), P("grp"))
    return jax.shard_map(
        functools.partial(local, mesh.shape["grp"], mesh.shape["fsdp"], chips_pair_groups(mesh)),
        mesh=mesh,
        in_specs=placed,
        out_specs=(P("grp", "fsdp", None), P("grp", "fsdp", None)),
        check_vma=False,
    )
```

```python
import functools
import math

import jax
import jax.numpy as jnp
from jax import lax
from jax.experimental import pallas as pl
from jax.experimental.pallas import tpu as pltpu
from jax.sharding import PartitionSpec as P

ITERS = 2

first_coef = 3.4445
second_coef = -4.775
third_coef = 2.0315

ROW_STEP = 16
SEND_COLS = 512
VMEM_BYTES = 63 * 1024 * 1024


def kernel(
    groups, size, paired,
    counts_hbm, grads_hbm, momentum_hbm, update_hbm, new_hbm,
    counts_ref, grads, momentum, fresh, owned, gram_out, gram_in, result, fsdp_sums, grp_sums,
    count_sem, load_sem, store_sem, own_sem,
    fsdp_send, fsdp_recv, grp_send, grp_recv,
    out_send, out_recv, gram_send, gram_recv, back_send, back_recv,
):
    matrices, rows, width = grads.shape
    half = width // 2
    step_cols = math.gcd(half, SEND_COLS)
    steps = half // step_cols
    f = lax.axis_index("fsdp")
    g = lax.axis_index("grp")

    def dev(a, b):
        return {"fsdp": a, "grp": b}

    if paired:
        core = lax.rem(g, 2)
        base = g - core
        owner_g = base + f // matrices
        owner_m = lax.rem(f, matrices)
        my_half = core
        peer = (f, base + 1 - core)

        def target(m, h):
            return core * matrices + m, base + h
    else:
        owner_g = g
        owner_m = f // 2
        my_half = lax.rem(f, 2)
        peer = (f + 1 - 2 * my_half, g)

        def target(m, h):
            return jnp.int32(2 * m + h), g

    barrier = pltpu.get_barrier_semaphore()
    others = [(lax.rem(f + d, size), g) for d in range(1, size)]
    others += [(f, lax.rem(g + d, groups)) for d in range(1, groups)]
    if paired:
        others += [(lax.rem(f + d, size), base + 1 - core) for d in range(1, size)]
    for a, b in others:
        pl.semaphore_signal(barrier, inc=1, device_id=dev(a, b), device_id_type=pl.DeviceIdType.MESH)

    load_counts = pltpu.make_async_copy(counts_hbm, counts_ref, count_sem)
    load_counts.start()
    piece = load_rows(rows)
    loads = [
        [
            pltpu.make_async_copy(
                source.at[m, pl.ds(r, piece), :], kept.at[m, pl.ds(r, piece), :],
                load_sem.at[k, m * (rows // piece) + r // piece],
            )
            for m in range(matrices)
            for r in range(0, rows, piece)
        ]
        for k, (source, kept) in enumerate(((grads_hbm, grads), (momentum_hbm, momentum)))
    ]
    for load in loads[0] + loads[1]:
        load.start()

    offset = f * rows

    def live_mask(m, r):
        ids = offset + r + lax.broadcasted_iota(jnp.int32, (ROW_STEP, 1), 0)
        return ids < counts_ref[m]

    load_counts.wait()
    acc = jnp.zeros((8, width), jnp.float32)
    for m in range(matrices):
        for r in range(0, rows, ROW_STEP):
            if r % piece == 0:
                loads[0][m * (rows // piece) + r // piece].wait()
            part = jnp.where(live_mask(m, r), grads[m, r:r + ROW_STEP, :].astype(jnp.float32), 0.0)
            part = part * part
            for k in range(0, ROW_STEP, 8):
                acc = acc + part[k:k + 8]
    tile = acc[:, :128]
    for k in range(128, width, 128):
        tile = tile + acc[:, k:k + 128]
    live_rows = jnp.int32(0)
    for m in range(matrices):
        live_rows = live_rows + jnp.clip(counts_ref[m] - offset, 0, rows)
    fsdp_sums[f, 0:8, :] = tile
    fsdp_sums[f, 8:16, :] = jnp.zeros((8, 128), jnp.float32) + live_rows.astype(jnp.float32)

    pl.semaphore_wait(barrier, len(others))

    def exchange(buf, me, count, place, send, recv):
        copies = []
        for d in range(1, count):
            a, b = place(lax.rem(me + d, count))
            copy = pltpu.make_async_remote_copy(
                buf.at[me], buf.at[me], send.at[d], recv.at[d],
                device_id=dev(a, b), device_id_type=pl.DeviceIdType.MESH,
            )
            copy.start()
            copies.append(copy)
        for copy in copies:
            copy.wait_recv()
        total = buf[0]
        for d in range(1, count):
            total = total + buf[d]
        return total, copies

    total, fsdp_copies = exchange(fsdp_sums, f, size, lambda i: (i, g), fsdp_send, fsdp_recv)
    grp_sums[g] = total
    for load in loads[1]:
        load.wait()
    total, grp_copies = exchange(grp_sums, g, groups, lambda i: (f, i), grp_send, grp_recv)
    square_sum = jnp.sum(total[0:8], keepdims=True)
    row_total = total[8:9, 0:1]
    clip = jnp.minimum(1.0, lax.rsqrt(square_sum / (row_total * width) + 1e-06))

    def out_copy(m, h):
        a, b = target(m, h)
        copy = pltpu.make_async_remote_copy(
            fresh.at[m, :, pl.ds(h * half, half)],
            owned.at[pl.ds(pl.multiple_of(f * rows, 16), rows), :],
            out_send.at[m * 2 + h], out_recv.at[f],
            device_id=dev(a, b), device_id_type=pl.DeviceIdType.MESH,
        )
        return copy, jnp.logical_and(a == f, b == g)

    for m in range(matrices):
        for h in range(2):
            cols = slice(h * half, (h + 1) * half)
            for r in range(0, rows, ROW_STEP):
                at = (m, slice(r, r + ROW_STEP), cols)
                fresh[at] = jnp.where(
                    live_mask(m, r),
                    0.95 * momentum[at].astype(jnp.float32) + clip * grads[at].astype(jnp.float32),
                    0.0,
                ).astype(jnp.bfloat16)
            copy, mine = out_copy(m, h)

            @pl.when(jnp.logical_not(mine))
            def _():
                copy.start()

            @pl.when(mine)
            def _():
                owned[pl.ds(pl.multiple_of(f * rows, 16), rows), :] = fresh[m, :, cols]

    store_new = pltpu.make_async_copy(fresh, new_hbm, store_sem)
    store_new.start()

    def here(i):
        return jnp.logical_and(i == f, owner_g == g)

    for i in range(size):
        arrive = pltpu.make_async_remote_copy(
            fresh.at[0, :, pl.ds(0, half)], owned.at[pl.ds(i * rows, rows), :],
            out_send.at[0], out_recv.at[i],
            device_id=dev(f, owner_g), device_id_type=pl.DeviceIdType.MESH,
        )

        @pl.when(jnp.logical_not(here(i)))
        def _():
            arrive.wait_recv()

    def dot(a, b):
        return jnp.dot(a.astype(jnp.bfloat16), b.astype(jnp.bfloat16), preferred_element_type=jnp.float32)

    full = owned[...]
    gram = lax.dot_general(full, full, (((1,), (1,)), ((), ())), preferred_element_type=jnp.float32)
    gram_out[...] = gram.astype(jnp.bfloat16)
    gram_copy = pltpu.make_async_remote_copy(
        gram_out, gram_in, gram_send, gram_recv,
        device_id=dev(*peer), device_id_type=pl.DeviceIdType.MESH,
    )
    gram_copy.start()
    gram_copy.wait_recv()
    gram = gram + gram_in[...].astype(jnp.float32)
    order = gram.shape[0]
    diagonal = lax.broadcasted_iota(jnp.int32, (order, order), 0) == lax.broadcasted_iota(
        jnp.int32, (order, order), 1
    )
    trace = jnp.sum(jnp.where(diagonal, gram, 0.0), keepdims=True)
    inverse = 1.0 / (jnp.sqrt(trace) + 1e-07)
    gram = (gram * inverse) * inverse
    poly = second_coef * gram + third_coef * dot(gram, gram)
    mix = poly
    for _ in range(ITERS - 1):
        turned = dot(poly, gram)
        gram = first_coef * first_coef * gram + 2 * first_coef * turned + dot(poly, turned)
        before = poly
        poly = second_coef * gram + third_coef * dot(gram, gram)
        mix = first_coef * (before + poly) + dot(poly, before)
    lead = first_coef ** ITERS
    mix = mix.astype(jnp.bfloat16)
    scale = inverse * (0.2 * math.sqrt(width))

    def back_copy(i, j):
        copy = pltpu.make_async_remote_copy(
            result.at[j, pl.ds(i * rows, rows), :],
            update_hbm.at[
                owner_m, :, pl.ds(pl.multiple_of(my_half * half + j * step_cols, step_cols), step_cols)
            ],
            back_send.at[i * steps + j],
            back_recv.at[(owner_m * 2 + my_half) * steps + j],
            device_id=dev(jnp.int32(i), owner_g), device_id_type=pl.DeviceIdType.MESH,
        )
        local = pltpu.make_async_copy(
            result.at[j, pl.ds(i * rows, rows), :],
            update_hbm.at[
                owner_m, :, pl.ds(pl.multiple_of(my_half * half + j * step_cols, step_cols), step_cols)
            ],
            own_sem.at[j],
        )
        return copy, local

    for j in range(steps):
        block = owned[:, j * step_cols:(j + 1) * step_cols]
        made = lead * block.astype(jnp.float32) + jnp.dot(mix, block, preferred_element_type=jnp.float32)
        result[j] = (scale * made).astype(jnp.bfloat16)
        for i in range(size):
            copy, local = back_copy(i, j)

            @pl.when(jnp.logical_not(here(i)))
            def _():
                copy.start()

            @pl.when(here(i))
            def _():
                local.start()

    for copy in fsdp_copies + grp_copies:
        copy.wait_send()
    gram_copy.wait_send()
    for m in range(matrices):
        for h in range(2):
            copy, mine = out_copy(m, h)

            @pl.when(jnp.logical_not(mine))
            def _():
                copy.wait_send()

    store_new.wait()
    for j in range(steps):
        for i in range(size):
            copy, local = back_copy(i, j)

            @pl.when(jnp.logical_not(here(i)))
            def _():
                copy.wait_send()

            @pl.when(here(i))
            def _():
                local.wait()

    for m in range(matrices):
        for h in range(2):
            a, b = target(m, h)
            for j in range(steps):
                arrive = pltpu.make_async_remote_copy(
                    result.at[j, pl.ds(0, rows), :],
                    update_hbm.at[m, :, pl.ds(h * half + j * step_cols, step_cols)],
                    back_send.at[0], back_recv.at[(m * 2 + h) * steps + j],
                    device_id=dev(a, b), device_id_type=pl.DeviceIdType.MESH,
                )

                @pl.when(jnp.logical_not(jnp.logical_and(a == f, b == g)))
                def _():
                    arrive.wait_recv()


def load_rows(rows):
    return 32 if rows % 32 == 0 else rows


def local(groups, size, paired, grads, momentum, row_counts):
    matrices, rows, width = grads.shape
    half = width // 2
    step_cols = math.gcd(half, SEND_COLS)
    steps = half // step_cols
    order = size * rows
    dma = pltpu.SemaphoreType.DMA
    update, new_momentum = pl.pallas_call(
        functools.partial(kernel, groups, size, paired),
        out_shape=(
            jax.ShapeDtypeStruct(grads.shape, jnp.bfloat16),
            jax.ShapeDtypeStruct(grads.shape, jnp.bfloat16),
        ),
        in_specs=[
            pl.BlockSpec(memory_space=pltpu.HBM),
            pl.BlockSpec(memory_space=pltpu.HBM),
            pl.BlockSpec(memory_space=pltpu.HBM),
        ],
        out_specs=(pl.BlockSpec(memory_space=pl.ANY), pl.BlockSpec(memory_space=pl.ANY)),
        scratch_shapes=[
            pltpu.SMEM(row_counts.shape, jnp.int32),
            pltpu.VMEM(grads.shape, jnp.bfloat16),
            pltpu.VMEM(grads.shape, jnp.bfloat16),
            pltpu.VMEM(grads.shape, jnp.bfloat16),
            pltpu.VMEM((order, half), jnp.bfloat16),
            pltpu.VMEM((order, order), jnp.bfloat16),
            pltpu.VMEM((order, order), jnp.bfloat16),
            pltpu.VMEM((steps, order, step_cols), jnp.bfloat16),
            pltpu.VMEM((size, 16, 128), jnp.float32),
            pltpu.VMEM((groups, 16, 128), jnp.float32),
            dma,
            dma((2, matrices * (rows // load_rows(rows)))),
            dma,
            dma((steps,)),
            dma((size,)),
            dma((size,)),
            dma((groups,)),
            dma((groups,)),
            dma((2 * matrices,)),
            dma((size,)),
            dma,
            dma,
            dma((size * steps,)),
            dma((2 * matrices * steps,)),
        ],
        compiler_params=pltpu.CompilerParams(
            collective_id=0, has_side_effects=True, vmem_limit_bytes=VMEM_BYTES
        ),
        cost_estimate=pl.CostEstimate(
            flops=4 * order * order * half, bytes_accessed=8 * grads.size, transcendentals=0
        ),
    )(row_counts, grads, momentum)
    return update, new_momentum


def chips_pair_groups(mesh):
    names = list(mesh.axis_names)
    grid = mesh.devices
    if names != ["fsdp", "grp"] or grid.shape[1] % 2:
        return False
    return all(
        getattr(grid[0, i], "coords", None) is not None
        and tuple(grid[0, i].coords) == tuple(grid[0, i + 1].coords)
        for i in range(0, grid.shape[1], 2)
    )


def solution(mesh):
    placed = (P("grp", "fsdp", None), P("grp", "fsdp", None), P("grp"))
    return jax.shard_map(
        functools.partial(local, mesh.shape["grp"], mesh.shape["fsdp"], chips_pair_groups(mesh)),
        mesh=mesh,
        in_specs=placed,
        out_specs=(P("grp", "fsdp", None), P("grp", "fsdp", None)),
        check_vma=False,
    )
```

```python
import functools
import math

import jax
import jax.numpy as jnp
from jax import lax
from jax.experimental import pallas as pl
from jax.experimental.pallas import tpu as pltpu
from jax.sharding import PartitionSpec as P

ITERS = 2

first_coef = 3.4445
second_coef = -4.775
third_coef = 2.0315

ROW_STEP = 16
SEND_COLS = 512
VMEM_BYTES = 63 * 1024 * 1024


def kernel(
    groups, size, paired,
    counts_hbm, grads_hbm, momentum_hbm, update_hbm, new_hbm,
    counts_ref, grads, momentum, fresh, owned, gram_out, gram_in, result, fsdp_sums, grp_sums,
    count_sem, load_sem, store_sem, own_sem,
    fsdp_send, fsdp_recv, grp_send, grp_recv,
    out_send, out_recv, gram_send, gram_recv, back_send, back_recv,
):
    matrices, rows, width = grads.shape
    half = width // 2
    step_cols = math.gcd(half, SEND_COLS)
    steps = half // step_cols
    f = lax.axis_index("fsdp")
    g = lax.axis_index("grp")

    def dev(a, b):
        return {"fsdp": a, "grp": b}

    if paired:
        core = lax.rem(g, 2)
        base = g - core
        owner_g = base + f // matrices
        owner_m = lax.rem(f, matrices)
        my_half = core
        peer = (f, base + 1 - core)

        def target(m, h):
            return core * matrices + m, base + h

        def nth(k):
            return jnp.where(core == 1, k, matrices - 1 - k)
    else:
        owner_g = g
        owner_m = f // 2
        my_half = lax.rem(f, 2)
        peer = (f + 1 - 2 * my_half, g)

        def target(m, h):
            return jnp.int32(2 * m + h), g

        def nth(k):
            return k

    barrier = pltpu.get_barrier_semaphore()
    others = [(lax.rem(f + d, size), g) for d in range(1, size)]
    others += [(f, lax.rem(g + d, groups)) for d in range(1, groups)]
    if paired:
        others += [(lax.rem(f + d, size), base + 1 - core) for d in range(1, size)]
    for a, b in others:
        pl.semaphore_signal(barrier, inc=1, device_id=dev(a, b), device_id_type=pl.DeviceIdType.MESH)

    load_counts = pltpu.make_async_copy(counts_hbm, counts_ref, count_sem)
    load_counts.start()
    piece = load_rows(rows)
    loads = [
        [
            pltpu.make_async_copy(
                source.at[m, pl.ds(r, piece), :], kept.at[m, pl.ds(r, piece), :],
                load_sem.at[k, m * (rows // piece) + r // piece],
            )
            for m in range(matrices)
            for r in range(0, rows, piece)
        ]
        for k, (source, kept) in enumerate(((grads_hbm, grads), (momentum_hbm, momentum)))
    ]
    for load in loads[0] + loads[1]:
        load.start()

    offset = f * rows

    def live_mask(m, r):
        ids = offset + r + lax.broadcasted_iota(jnp.int32, (ROW_STEP, 1), 0)
        return ids < counts_ref[m]

    load_counts.wait()
    acc = jnp.zeros((8, width), jnp.float32)
    for m in range(matrices):
        for r in range(0, rows, ROW_STEP):
            if r % piece == 0:
                loads[0][m * (rows // piece) + r // piece].wait()
            part = jnp.where(live_mask(m, r), grads[m, r:r + ROW_STEP, :].astype(jnp.float32), 0.0)
            part = part * part
            for k in range(0, ROW_STEP, 8):
                acc = acc + part[k:k + 8]
    tile = acc[:, :128]
    for k in range(128, width, 128):
        tile = tile + acc[:, k:k + 128]
    live_rows = jnp.int32(0)
    for m in range(matrices):
        live_rows = live_rows + jnp.clip(counts_ref[m] - offset, 0, rows)
    fsdp_sums[f, 0:8, :] = tile
    fsdp_sums[f, 8:16, :] = jnp.zeros((8, 128), jnp.float32) + live_rows.astype(jnp.float32)

    pl.semaphore_wait(barrier, len(others))

    def exchange(buf, me, count, place, send, recv):
        copies = []
        for d in range(1, count):
            a, b = place(lax.rem(me + d, count))
            copy = pltpu.make_async_remote_copy(
                buf.at[me], buf.at[me], send.at[d], recv.at[d],
                device_id=dev(a, b), device_id_type=pl.DeviceIdType.MESH,
            )
            copy.start()
            copies.append(copy)
        for copy in copies:
            copy.wait_recv()
        total = buf[0]
        for d in range(1, count):
            total = total + buf[d]
        return total, copies

    total, fsdp_copies = exchange(fsdp_sums, f, size, lambda i: (i, g), fsdp_send, fsdp_recv)
    grp_sums[g] = total
    for load in loads[1]:
        load.wait()
    total, grp_copies = exchange(grp_sums, g, groups, lambda i: (f, i), grp_send, grp_recv)
    square_sum = jnp.sum(total[0:8], keepdims=True)
    row_total = total[8:9, 0:1]
    clip = jnp.minimum(1.0, lax.rsqrt(square_sum / (row_total * width) + 1e-06))

    def out_copy(k, h):
        m = nth(k)
        a, b = target(m, h)
        copy = pltpu.make_async_remote_copy(
            fresh.at[m, :, pl.ds(h * half, half)],
            owned.at[pl.ds(pl.multiple_of(f * rows, 16), rows), :],
            out_send.at[k * 2 + h], out_recv.at[f],
            device_id=dev(a, b), device_id_type=pl.DeviceIdType.MESH,
        )
        return copy, jnp.logical_and(a == f, b == g)

    def wait_out(k):
        for h in range(2):
            copy, mine = out_copy(k, h)

            @pl.when(jnp.logical_not(mine))
            def _():
                copy.wait_send()

    for k in range(matrices):
        m = nth(k)
        for h in range(2):
            cols = slice(h * half, (h + 1) * half)
            for r in range(0, rows, ROW_STEP):
                at = (m, slice(r, r + ROW_STEP), cols)
                fresh[at] = jnp.where(
                    live_mask(m, r),
                    0.95 * momentum[at].astype(jnp.float32) + clip * grads[at].astype(jnp.float32),
                    0.0,
                ).astype(jnp.bfloat16)
        if k:
            wait_out(k - 1)
        for h in range(2):
            copy, mine = out_copy(k, h)

            @pl.when(jnp.logical_not(mine))
            def _():
                copy.start()

            @pl.when(mine)
            def _():
                cols = slice(h * half, (h + 1) * half)
                owned[pl.ds(pl.multiple_of(f * rows, 16), rows), :] = fresh[m, :, cols]

    store_new = pltpu.make_async_copy(fresh, new_hbm, store_sem)
    store_new.start()

    def here(i):
        return jnp.logical_and(i == f, owner_g == g)

    for i in range(size):
        arrive = pltpu.make_async_remote_copy(
            fresh.at[0, :, pl.ds(0, half)], owned.at[pl.ds(i * rows, rows), :],
            out_send.at[0], out_recv.at[i],
            device_id=dev(f, owner_g), device_id_type=pl.DeviceIdType.MESH,
        )

        @pl.when(jnp.logical_not(here(i)))
        def _():
            arrive.wait_recv()

    def dot(a, b):
        return jnp.dot(a.astype(jnp.bfloat16), b.astype(jnp.bfloat16), preferred_element_type=jnp.float32)

    full = owned[...]
    gram = lax.dot_general(full, full, (((1,), (1,)), ((), ())), preferred_element_type=jnp.float32)
    gram_out[...] = gram.astype(jnp.bfloat16)
    gram_copy = pltpu.make_async_remote_copy(
        gram_out, gram_in, gram_send, gram_recv,
        device_id=dev(*peer), device_id_type=pl.DeviceIdType.MESH,
    )
    gram_copy.start()
    gram_copy.wait_recv()
    gram = gram + gram_in[...].astype(jnp.float32)
    order = gram.shape[0]
    diagonal = lax.broadcasted_iota(jnp.int32, (order, order), 0) == lax.broadcasted_iota(
        jnp.int32, (order, order), 1
    )
    trace = jnp.sum(jnp.where(diagonal, gram, 0.0), keepdims=True)
    inverse = 1.0 / (jnp.sqrt(trace) + 1e-07)
    gram = (gram * inverse) * inverse
    poly = second_coef * gram + third_coef * dot(gram, gram)
    mix = poly
    for _ in range(ITERS - 1):
        turned = dot(poly, gram)
        gram = first_coef * first_coef * gram + 2 * first_coef * turned + dot(poly, turned)
        before = poly
        poly = second_coef * gram + third_coef * dot(gram, gram)
        mix = first_coef * (before + poly) + dot(poly, before)
    lead = first_coef ** ITERS
    mix = mix.astype(jnp.bfloat16)
    scale = inverse * (0.2 * math.sqrt(width))

    def back_to(d):
        return jnp.where(f < size // 2, size - 1 - d, d)

    def back_copy(d, j):
        i = back_to(d)
        copy = pltpu.make_async_remote_copy(
            result.at[j, pl.ds(pl.multiple_of(i * rows, 16), rows), :],
            update_hbm.at[
                owner_m, :, pl.ds(pl.multiple_of(my_half * half + j * step_cols, step_cols), step_cols)
            ],
            back_send.at[d * steps + j],
            back_recv.at[(owner_m * 2 + my_half) * steps + j],
            device_id=dev(i, owner_g), device_id_type=pl.DeviceIdType.MESH,
        )
        local = pltpu.make_async_copy(
            result.at[j, pl.ds(pl.multiple_of(i * rows, 16), rows), :],
            update_hbm.at[
                owner_m, :, pl.ds(pl.multiple_of(my_half * half + j * step_cols, step_cols), step_cols)
            ],
            own_sem.at[j],
        )
        return copy, local

    for j in range(steps):
        block = owned[:, j * step_cols:(j + 1) * step_cols]
        made = lead * block.astype(jnp.float32) + jnp.dot(mix, block, preferred_element_type=jnp.float32)
        result[j] = (scale * made).astype(jnp.bfloat16)
        for d in range(size):
            copy, local = back_copy(d, j)

            @pl.when(jnp.logical_not(here(back_to(d))))
            def _():
                copy.start()

            @pl.when(here(back_to(d)))
            def _():
                local.start()

    for copy in fsdp_copies + grp_copies:
        copy.wait_send()
    gram_copy.wait_send()
    wait_out(matrices - 1)
    store_new.wait()
    for j in range(steps):
        for d in range(size):
            copy, local = back_copy(d, j)

            @pl.when(jnp.logical_not(here(back_to(d))))
            def _():
                copy.wait_send()

            @pl.when(here(back_to(d)))
            def _():
                local.wait()

    for m in range(matrices):
        for h in range(2):
            a, b = target(m, h)
            for j in range(steps):
                arrive = pltpu.make_async_remote_copy(
                    result.at[j, pl.ds(0, rows), :],
                    update_hbm.at[m, :, pl.ds(h * half + j * step_cols, step_cols)],
                    back_send.at[0], back_recv.at[(m * 2 + h) * steps + j],
                    device_id=dev(a, b), device_id_type=pl.DeviceIdType.MESH,
                )

                @pl.when(jnp.logical_not(jnp.logical_and(a == f, b == g)))
                def _():
                    arrive.wait_recv()


def load_rows(rows):
    return 32 if rows % 32 == 0 else rows


def local(groups, size, paired, grads, momentum, row_counts):
    matrices, rows, width = grads.shape
    half = width // 2
    step_cols = math.gcd(half, SEND_COLS)
    steps = half // step_cols
    order = size * rows
    dma = pltpu.SemaphoreType.DMA
    update, new_momentum = pl.pallas_call(
        functools.partial(kernel, groups, size, paired),
        out_shape=(
            jax.ShapeDtypeStruct(grads.shape, jnp.bfloat16),
            jax.ShapeDtypeStruct(grads.shape, jnp.bfloat16),
        ),
        in_specs=[
            pl.BlockSpec(memory_space=pltpu.HBM),
            pl.BlockSpec(memory_space=pltpu.HBM),
            pl.BlockSpec(memory_space=pltpu.HBM),
        ],
        out_specs=(pl.BlockSpec(memory_space=pl.ANY), pl.BlockSpec(memory_space=pl.ANY)),
        scratch_shapes=[
            pltpu.SMEM(row_counts.shape, jnp.int32),
            pltpu.VMEM(grads.shape, jnp.bfloat16),
            pltpu.VMEM(grads.shape, jnp.bfloat16),
            pltpu.VMEM(grads.shape, jnp.bfloat16),
            pltpu.VMEM((order, half), jnp.bfloat16),
            pltpu.VMEM((order, order), jnp.bfloat16),
            pltpu.VMEM((order, order), jnp.bfloat16),
            pltpu.VMEM((steps, order, step_cols), jnp.bfloat16),
            pltpu.VMEM((size, 16, 128), jnp.float32),
            pltpu.VMEM((groups, 16, 128), jnp.float32),
            dma,
            dma((2, matrices * (rows // load_rows(rows)))),
            dma,
            dma((steps,)),
            dma((size,)),
            dma((size,)),
            dma((groups,)),
            dma((groups,)),
            dma((2 * matrices,)),
            dma((size,)),
            dma,
            dma,
            dma((size * steps,)),
            dma((2 * matrices * steps,)),
        ],
        compiler_params=pltpu.CompilerParams(
            collective_id=0, has_side_effects=True, vmem_limit_bytes=VMEM_BYTES
        ),
        cost_estimate=pl.CostEstimate(
            flops=4 * order * order * half, bytes_accessed=8 * grads.size, transcendentals=0
        ),
    )(row_counts, grads, momentum)
    return update, new_momentum


def chips_pair_groups(mesh):
    names = list(mesh.axis_names)
    grid = mesh.devices
    if names != ["fsdp", "grp"] or grid.shape[1] % 2:
        return False
    return all(
        getattr(grid[0, i], "coords", None) is not None
        and tuple(grid[0, i].coords) == tuple(grid[0, i + 1].coords)
        for i in range(0, grid.shape[1], 2)
    )


def solution(mesh):
    placed = (P("grp", "fsdp", None), P("grp", "fsdp", None), P("grp"))
    return jax.shard_map(
        functools.partial(local, mesh.shape["grp"], mesh.shape["fsdp"], chips_pair_groups(mesh)),
        mesh=mesh,
        in_specs=placed,
        out_specs=(P("grp", "fsdp", None), P("grp", "fsdp", None)),
        check_vma=False,
    )
```

```python
import functools
import math

import jax
import jax.numpy as jnp
from jax import lax
from jax.experimental import pallas as pl
from jax.experimental.pallas import tpu as pltpu
from jax.sharding import PartitionSpec as P

ITERS = 2

first_coef = 3.4445
second_coef = -4.775
third_coef = 2.0315

ROW_STEP = 16
SEND_COLS = 512
VMEM_BYTES = 40 * 1024 * 1024


def kernel(
    groups, size, paired,
    counts_hbm, grads_hbm, momentum_hbm, update_hbm, new_hbm,
    counts_ref, grads, momentum, fresh, owned, gram_out, gram_in, result, fsdp_sums, grp_sums,
    count_sem, load_sem, store_sem, own_sem,
    fsdp_send, fsdp_recv, grp_send, grp_recv,
    out_send, out_recv, gram_send, gram_recv, back_send, back_recv,
):
    matrices, rows, width = grads.shape
    half = width // 2
    step_cols = math.gcd(half, SEND_COLS)
    steps = half // step_cols
    f = lax.axis_index("fsdp")
    g = lax.axis_index("grp")

    def dev(a, b):
        return {"fsdp": a, "grp": b}

    if paired:
        core = lax.rem(g, 2)
        base = g - core
        owner_g = base + f // matrices
        owner_m = lax.rem(f, matrices)
        my_half = core
        peer = (f, base + 1 - core)

        def target(m, h):
            return core * matrices + m, base + h
    else:
        owner_g = g
        owner_m = f // 2
        my_half = lax.rem(f, 2)
        peer = (f + 1 - 2 * my_half, g)

        def target(m, h):
            return jnp.int32(2 * m + h), g

    barrier = pltpu.get_barrier_semaphore()
    others = [(lax.rem(f + d, size), g) for d in range(1, size)]
    others += [(f, lax.rem(g + d, groups)) for d in range(1, groups)]
    if paired:
        others += [(lax.rem(f + d, size), base + 1 - core) for d in range(1, size)]
    for a, b in others:
        pl.semaphore_signal(barrier, inc=1, device_id=dev(a, b), device_id_type=pl.DeviceIdType.MESH)

    load_counts = pltpu.make_async_copy(counts_hbm, counts_ref, count_sem)
    load_counts.start()
    piece = load_rows(rows)
    loads = [
        [
            pltpu.make_async_copy(
                source.at[m, pl.ds(r, piece), :], kept.at[m, pl.ds(r, piece), :],
                load_sem.at[k, m * (rows // piece) + r // piece],
            )
            for m in range(matrices)
            for r in range(0, rows, piece)
        ]
        for k, (source, kept) in enumerate(((grads_hbm, grads), (momentum_hbm, momentum)))
    ]
    for load in loads[0] + loads[1]:
        load.start()

    offset = f * rows

    def live_mask(m, r):
        ids = offset + r + lax.broadcasted_iota(jnp.int32, (ROW_STEP, 1), 0)
        return ids < counts_ref[m]

    load_counts.wait()
    acc = jnp.zeros((8, width), jnp.float32)
    for m in range(matrices):
        for r in range(0, rows, ROW_STEP):
            if r % piece == 0:
                loads[0][m * (rows // piece) + r // piece].wait()
            part = jnp.where(live_mask(m, r), grads[m, r:r + ROW_STEP, :].astype(jnp.float32), 0.0)
            part = part * part
            for k in range(0, ROW_STEP, 8):
                acc = acc + part[k:k + 8]
    tile = acc[:, :128]
    for k in range(128, width, 128):
        tile = tile + acc[:, k:k + 128]
    live_rows = jnp.int32(0)
    for m in range(matrices):
        live_rows = live_rows + jnp.clip(counts_ref[m] - offset, 0, rows)
    fsdp_sums[f, 0:8, :] = tile
    fsdp_sums[f, 8:16, :] = jnp.zeros((8, 128), jnp.float32) + live_rows.astype(jnp.float32)

    pl.semaphore_wait(barrier, len(others))

    def exchange(buf, me, count, place, send, recv):
        copies = []
        for d in range(1, count):
            a, b = place(lax.rem(me + d, count))
            copy = pltpu.make_async_remote_copy(
                buf.at[me], buf.at[me], send.at[d], recv.at[d],
                device_id=dev(a, b), device_id_type=pl.DeviceIdType.MESH,
            )
            copy.start()
            copies.append(copy)
        for copy in copies:
            copy.wait_recv()
        total = buf[0]
        for d in range(1, count):
            total = total + buf[d]
        return total, copies

    total, fsdp_copies = exchange(fsdp_sums, f, size, lambda i: (i, g), fsdp_send, fsdp_recv)
    grp_sums[g] = total
    for load in loads[1]:
        load.wait()
    total, grp_copies = exchange(grp_sums, g, groups, lambda i: (f, i), grp_send, grp_recv)
    square_sum = jnp.sum(total[0:8], keepdims=True)
    row_total = total[8:9, 0:1]
    clip = jnp.minimum(1.0, lax.rsqrt(square_sum / (row_total * width) + 1e-06))

    def out_copy(m, h):
        a, b = target(m, h)
        copy = pltpu.make_async_remote_copy(
            fresh.at[m, :, pl.ds(h * half, half)],
            owned.at[pl.ds(pl.multiple_of(f * rows, 16), rows), :],
            out_send.at[m * 2 + h], out_recv.at[f],
            device_id=dev(a, b), device_id_type=pl.DeviceIdType.MESH,
        )
        return copy, jnp.logical_and(a == f, b == g)

    for m in range(matrices):
        for h in range(2):
            cols = slice(h * half, (h + 1) * half)
            for r in range(0, rows, ROW_STEP):
                at = (m, slice(r, r + ROW_STEP), cols)
                fresh[at] = jnp.where(
                    live_mask(m, r),
                    0.95 * momentum[at].astype(jnp.float32) + clip * grads[at].astype(jnp.float32),
                    0.0,
                ).astype(jnp.bfloat16)
            copy, mine = out_copy(m, h)

            @pl.when(jnp.logical_not(mine))
            def _():
                copy.start()

            @pl.when(mine)
            def _():
                owned[pl.ds(pl.multiple_of(f * rows, 16), rows), :] = fresh[m, :, cols]

    store_new = pltpu.make_async_copy(fresh, new_hbm, store_sem)
    store_new.start()

    def here(i):
        return jnp.logical_and(i == f, owner_g == g)

    for i in range(size):
        arrive = pltpu.make_async_remote_copy(
            fresh.at[0, :, pl.ds(0, half)], owned.at[pl.ds(i * rows, rows), :],
            out_send.at[0], out_recv.at[i],
            device_id=dev(f, owner_g), device_id_type=pl.DeviceIdType.MESH,
        )

        @pl.when(jnp.logical_not(here(i)))
        def _():
            arrive.wait_recv()

    def dot(a, b):
        return jnp.dot(a.astype(jnp.bfloat16), b.astype(jnp.bfloat16), preferred_element_type=jnp.float32)

    full = owned[...]
    gram = lax.dot_general(full, full, (((1,), (1,)), ((), ())), preferred_element_type=jnp.float32)
    gram_out[...] = gram.astype(jnp.bfloat16)
    gram_copy = pltpu.make_async_remote_copy(
        gram_out, gram_in, gram_send, gram_recv,
        device_id=dev(*peer), device_id_type=pl.DeviceIdType.MESH,
    )
    gram_copy.start()
    gram_copy.wait_recv()
    gram = gram + gram_in[...].astype(jnp.float32)
    order = gram.shape[0]
    diagonal = lax.broadcasted_iota(jnp.int32, (order, order), 0) == lax.broadcasted_iota(
        jnp.int32, (order, order), 1
    )
    trace = jnp.sum(jnp.where(diagonal, gram, 0.0), keepdims=True)
    inverse = 1.0 / (jnp.sqrt(trace) + 1e-07)
    gram = (gram * inverse) * inverse
    poly = second_coef * gram + third_coef * dot(gram, gram)
    mix = poly
    for _ in range(ITERS - 1):
        turned = dot(poly, gram)
        gram = first_coef * first_coef * gram + 2 * first_coef * turned + dot(poly, turned)
        before = poly
        poly = second_coef * gram + third_coef * dot(gram, gram)
        mix = first_coef * (before + poly) + dot(poly, before)
    lead = first_coef ** ITERS
    mix = mix.astype(jnp.bfloat16)
    scale = inverse * (0.2 * math.sqrt(width))

    def back_copy(i, j):
        copy = pltpu.make_async_remote_copy(
            result.at[j, pl.ds(i * rows, rows), :],
            update_hbm.at[
                owner_m, :, pl.ds(pl.multiple_of(my_half * half + j * step_cols, step_cols), step_cols)
            ],
            back_send.at[i * steps + j],
            back_recv.at[(owner_m * 2 + my_half) * steps + j],
            device_id=dev(jnp.int32(i), owner_g), device_id_type=pl.DeviceIdType.MESH,
        )
        local = pltpu.make_async_copy(
            result.at[j, pl.ds(i * rows, rows), :],
            update_hbm.at[
                owner_m, :, pl.ds(pl.multiple_of(my_half * half + j * step_cols, step_cols), step_cols)
            ],
            own_sem.at[j],
        )
        return copy, local

    for j in range(steps):
        block = owned[:, j * step_cols:(j + 1) * step_cols]
        made = lead * block.astype(jnp.float32) + jnp.dot(mix, block, preferred_element_type=jnp.float32)
        result[j] = (scale * made).astype(jnp.bfloat16)
        for i in range(size):
            copy, local = back_copy(i, j)

            @pl.when(jnp.logical_not(here(i)))
            def _():
                copy.start()

            @pl.when(here(i))
            def _():
                local.start()

    for copy in fsdp_copies + grp_copies:
        copy.wait_send()
    gram_copy.wait_send()
    for m in range(matrices):
        for h in range(2):
            copy, mine = out_copy(m, h)

            @pl.when(jnp.logical_not(mine))
            def _():
                copy.wait_send()

    store_new.wait()
    for j in range(steps):
        for i in range(size):
            copy, local = back_copy(i, j)

            @pl.when(jnp.logical_not(here(i)))
            def _():
                copy.wait_send()

            @pl.when(here(i))
            def _():
                local.wait()

    for m in range(matrices):
        for h in range(2):
            a, b = target(m, h)
            for j in range(steps):
                arrive = pltpu.make_async_remote_copy(
                    result.at[j, pl.ds(0, rows), :],
                    update_hbm.at[m, :, pl.ds(h * half + j * step_cols, step_cols)],
                    back_send.at[0], back_recv.at[(m * 2 + h) * steps + j],
                    device_id=dev(a, b), device_id_type=pl.DeviceIdType.MESH,
                )

                @pl.when(jnp.logical_not(jnp.logical_and(a == f, b == g)))
                def _():
                    arrive.wait_recv()


def load_rows(rows):
    return 32 if rows % 32 == 0 else rows


def store(update, new, update_hbm, new_hbm, sems):
    copies = [
        pltpu.make_async_copy(source.at[m], kept.at[m], sems.at[k, m])
        for k, (source, kept) in enumerate(((update, update_hbm), (new, new_hbm)))
        for m in range(update.shape[0])
    ]
    for copy in copies:
        copy.start()
    for copy in copies:
        copy.wait()


def local(groups, size, paired, grads, momentum, row_counts):
    matrices, rows, width = grads.shape
    half = width // 2
    step_cols = math.gcd(half, SEND_COLS)
    steps = half // step_cols
    order = size * rows
    dma = pltpu.SemaphoreType.DMA
    grads, momentum, row_counts = (
        pltpu.with_memory_space_constraint(value, pltpu.HBM) for value in (grads, momentum, row_counts)
    )
    update, new_momentum = pl.pallas_call(
        functools.partial(kernel, groups, size, paired),
        out_shape=(
            jax.ShapeDtypeStruct(grads.shape, jnp.bfloat16),
            jax.ShapeDtypeStruct(grads.shape, jnp.bfloat16),
        ),
        in_specs=[
            pl.BlockSpec(memory_space=pltpu.HBM),
            pl.BlockSpec(memory_space=pltpu.HBM),
            pl.BlockSpec(memory_space=pltpu.HBM),
        ],
        out_specs=(pl.BlockSpec(memory_space=pl.ANY), pl.BlockSpec(memory_space=pl.ANY)),
        scratch_shapes=[
            pltpu.SMEM(row_counts.shape, jnp.int32),
            pltpu.VMEM(grads.shape, jnp.bfloat16),
            pltpu.VMEM(grads.shape, jnp.bfloat16),
            pltpu.VMEM(grads.shape, jnp.bfloat16),
            pltpu.VMEM((order, half), jnp.bfloat16),
            pltpu.VMEM((order, order), jnp.bfloat16),
            pltpu.VMEM((order, order), jnp.bfloat16),
            pltpu.VMEM((steps, order, step_cols), jnp.bfloat16),
            pltpu.VMEM((size, 16, 128), jnp.float32),
            pltpu.VMEM((groups, 16, 128), jnp.float32),
            dma,
            dma((2, matrices * (rows // load_rows(rows)))),
            dma,
            dma((steps,)),
            dma((size,)),
            dma((size,)),
            dma((groups,)),
            dma((groups,)),
            dma((2 * matrices,)),
            dma((size,)),
            dma,
            dma,
            dma((size * steps,)),
            dma((2 * matrices * steps,)),
        ],
        compiler_params=pltpu.CompilerParams(
            collective_id=0, has_side_effects=True, vmem_limit_bytes=VMEM_BYTES
        ),
        cost_estimate=pl.CostEstimate(
            flops=4 * order * order * half, bytes_accessed=8 * grads.size, transcendentals=0
        ),
    )(row_counts, grads, momentum)
    return pl.pallas_call(
        store,
        out_shape=(
            jax.ShapeDtypeStruct(grads.shape, jnp.bfloat16),
            jax.ShapeDtypeStruct(grads.shape, jnp.bfloat16),
        ),
        in_specs=[pl.BlockSpec(memory_space=pl.ANY)] * 2,
        out_specs=(pl.BlockSpec(memory_space=pltpu.HBM), pl.BlockSpec(memory_space=pltpu.HBM)),
        scratch_shapes=[dma((2, matrices))],
        compiler_params=pltpu.CompilerParams(vmem_limit_bytes=VMEM_BYTES),
    )(update, new_momentum)


def chips_pair_groups(mesh):
    names = list(mesh.axis_names)
    grid = mesh.devices
    if names != ["fsdp", "grp"] or grid.shape[1] % 2:
        return False
    return all(
        getattr(grid[0, i], "coords", None) is not None
        and tuple(grid[0, i].coords) == tuple(grid[0, i + 1].coords)
        for i in range(0, grid.shape[1], 2)
    )


def solution(mesh):
    placed = (P("grp", "fsdp", None), P("grp", "fsdp", None), P("grp"))
    return jax.shard_map(
        functools.partial(local, mesh.shape["grp"], mesh.shape["fsdp"], chips_pair_groups(mesh)),
        mesh=mesh,
        in_specs=placed,
        out_specs=(P("grp", "fsdp", None), P("grp", "fsdp", None)),
        check_vma=False,
    )
```

```python
import functools
import math

import jax
import jax.numpy as jnp
from jax import lax
from jax.experimental import pallas as pl
from jax.experimental.pallas import tpu as pltpu
from jax.sharding import PartitionSpec as P

ITERS = 2

first_coef = 3.4445
second_coef = -4.775
third_coef = 2.0315

ROW_STEP = 16
SEND_COLS = 512
RAW_COLS = 128
VMEM_BYTES = 40 * 1024 * 1024


def kernel(
    groups, size, paired,
    counts_hbm, grads_hbm, momentum_hbm, update_hbm, new_hbm,
    counts_ref, grads, momentum, fresh, owned, raw_out, raw_in, gram_out, gram_in, result, fsdp_sums, grp_sums,
    count_sem, load_sem, store_sem, own_sem,
    fsdp_send, fsdp_recv, grp_send, grp_recv,
    raw_send, raw_recv, out_send, out_recv, gram_send, gram_recv, back_send, back_recv,
):
    matrices, rows, width = grads.shape
    half = width // 2
    step_cols = math.gcd(half, SEND_COLS)
    steps = half // step_cols
    f = lax.axis_index("fsdp")
    g = lax.axis_index("grp")

    def dev(a, b):
        return {"fsdp": a, "grp": b}

    if paired:
        core = lax.rem(g, 2)
        base = g - core
        owner_g = base + f // matrices
        owner_m = lax.rem(f, matrices)
        my_half = core
        peer = (f, base + 1 - core)

        def target(m, h):
            return core * matrices + m, base + h
    else:
        owner_g = g
        owner_m = f // 2
        my_half = lax.rem(f, 2)
        peer = (f + 1 - 2 * my_half, g)

        def target(m, h):
            return jnp.int32(2 * m + h), g

    barrier = pltpu.get_barrier_semaphore()
    others = [(lax.rem(f + d, size), g) for d in range(1, size)]
    others += [(f, lax.rem(g + d, groups)) for d in range(1, groups)]
    if paired:
        others += [(lax.rem(f + d, size), base + 1 - core) for d in range(1, size)]
    for a, b in others:
        pl.semaphore_signal(barrier, inc=1, device_id=dev(a, b), device_id_type=pl.DeviceIdType.MESH)

    load_counts = pltpu.make_async_copy(counts_hbm, counts_ref, count_sem)
    load_counts.start()
    piece = load_rows(rows)
    loads = [
        [
            pltpu.make_async_copy(
                source.at[m, pl.ds(r, piece), :], kept.at[m, pl.ds(r, piece), :],
                load_sem.at[k, m * (rows // piece) + r // piece],
            )
            for m in range(matrices)
            for r in range(0, rows, piece)
        ]
        for k, (source, kept) in enumerate(((grads_hbm, grads), (momentum_hbm, momentum)))
    ]
    for load in loads[0] + loads[1]:
        load.start()

    offset = f * rows

    def live_mask(m, r):
        ids = offset + r + lax.broadcasted_iota(jnp.int32, (ROW_STEP, 1), 0)
        return ids < counts_ref[m]

    load_counts.wait()
    acc = jnp.zeros((8, width), jnp.float32)
    for m in range(matrices):
        for r in range(0, rows, ROW_STEP):
            if r % piece == 0:
                loads[0][m * (rows // piece) + r // piece].wait()
            part = jnp.where(live_mask(m, r), grads[m, r:r + ROW_STEP, :].astype(jnp.float32), 0.0)
            part = part * part
            for k in range(0, ROW_STEP, 8):
                acc = acc + part[k:k + 8]
    tile = acc[:, :128]
    for k in range(128, width, 128):
        tile = tile + acc[:, k:k + 128]
    live_rows = jnp.int32(0)
    for m in range(matrices):
        live_rows = live_rows + jnp.clip(counts_ref[m] - offset, 0, rows)
    fsdp_sums[f, 0:8, :] = tile
    fsdp_sums[f, 8:16, :] = jnp.zeros((8, 128), jnp.float32) + live_rows.astype(jnp.float32)

    pl.semaphore_wait(barrier, len(others))

    def exchange(buf, me, count, place, send, recv):
        copies = []
        for d in range(1, count):
            a, b = place(lax.rem(me + d, count))
            copy = pltpu.make_async_remote_copy(
                buf.at[me], buf.at[me], send.at[d], recv.at[d],
                device_id=dev(a, b), device_id_type=pl.DeviceIdType.MESH,
            )
            copy.start()
            copies.append(copy)
        return copies

    def added(buf, copies):
        for copy in copies:
            copy.wait_recv()
        total = buf[0]
        for d in range(1, buf.shape[0]):
            total = total + buf[d]
        return total

    def raw_copy(m, h):
        a, b = target(m, h)
        copy = pltpu.make_async_remote_copy(
            raw_out.at[m, h],
            raw_in.at[:, pl.ds(pl.multiple_of(f * rows, 16), rows), :],
            raw_send.at[m * 2 + h], raw_recv.at[f],
            device_id=dev(a, b), device_id_type=pl.DeviceIdType.MESH,
        )
        return copy, jnp.logical_and(a == f, b == g)

    fsdp_copies = exchange(fsdp_sums, f, size, lambda i: (i, g), fsdp_send, fsdp_recv)
    for load in loads[1]:
        load.wait()
    for m in range(matrices):
        for h in range(2):
            for r in range(0, rows, ROW_STEP):
                live = live_mask(m, r)
                for k, kept in enumerate((grads, momentum)):
                    value = kept[m, r:r + ROW_STEP, h * half:h * half + RAW_COLS].astype(jnp.float32)
                    raw_out[m, h, k, r:r + ROW_STEP, :] = jnp.where(live, value, 0.0).astype(jnp.bfloat16)
            copy, mine = raw_copy(m, h)

            @pl.when(jnp.logical_not(mine))
            def _():
                copy.start()

    grp_sums[g] = added(fsdp_sums, fsdp_copies)
    grp_copies = exchange(grp_sums, g, groups, lambda i: (f, i), grp_send, grp_recv)
    total = added(grp_sums, grp_copies)
    square_sum = jnp.sum(total[0:8], keepdims=True)
    row_total = total[8:9, 0:1]
    clip = jnp.minimum(1.0, lax.rsqrt(square_sum / (row_total * width) + 1e-06))

    def out_copy(m, h):
        a, b = target(m, h)
        copy = pltpu.make_async_remote_copy(
            fresh.at[m, :, pl.ds(h * half + RAW_COLS, half - RAW_COLS)],
            owned.at[pl.ds(pl.multiple_of(f * rows, 16), rows), pl.ds(RAW_COLS, half - RAW_COLS)],
            out_send.at[m * 2 + h], out_recv.at[f],
            device_id=dev(a, b), device_id_type=pl.DeviceIdType.MESH,
        )
        return copy, jnp.logical_and(a == f, b == g)

    for m in range(matrices):
        for h in range(2):
            cols = slice(h * half, (h + 1) * half)
            for r in range(0, rows, ROW_STEP):
                at = (m, slice(r, r + ROW_STEP), cols)
                fresh[at] = jnp.where(
                    live_mask(m, r),
                    0.95 * momentum[at].astype(jnp.float32) + clip * grads[at].astype(jnp.float32),
                    0.0,
                ).astype(jnp.bfloat16)
            copy, mine = out_copy(m, h)

            @pl.when(jnp.logical_not(mine))
            def _():
                copy.start()

            @pl.when(mine)
            def _():
                owned[pl.ds(pl.multiple_of(f * rows, 16), rows), :] = fresh[m, :, cols]

    store_new = pltpu.make_async_copy(fresh, new_hbm, store_sem)
    store_new.start()

    def here(i):
        return jnp.logical_and(i == f, owner_g == g)

    for i in range(size):
        raw_arrive = pltpu.make_async_remote_copy(
            raw_out.at[0, 0], raw_in.at[:, pl.ds(i * rows, rows), :],
            raw_send.at[0], raw_recv.at[i],
            device_id=dev(f, owner_g), device_id_type=pl.DeviceIdType.MESH,
        )

        @pl.when(jnp.logical_not(here(i)))
        def _():
            raw_arrive.wait_recv()
            for r in range(i * rows, (i + 1) * rows, ROW_STEP):
                owned[r:r + ROW_STEP, 0:RAW_COLS] = (
                    0.95 * raw_in[1, r:r + ROW_STEP, :].astype(jnp.float32)
                    + clip * raw_in[0, r:r + ROW_STEP, :].astype(jnp.float32)
                ).astype(jnp.bfloat16)

    for i in range(size):
        arrive = pltpu.make_async_remote_copy(
            fresh.at[0, :, pl.ds(RAW_COLS, half - RAW_COLS)],
            owned.at[pl.ds(i * rows, rows), pl.ds(RAW_COLS, half - RAW_COLS)],
            out_send.at[0], out_recv.at[i],
            device_id=dev(f, owner_g), device_id_type=pl.DeviceIdType.MESH,
        )

        @pl.when(jnp.logical_not(here(i)))
        def _():
            arrive.wait_recv()

    def dot(a, b):
        return jnp.dot(a.astype(jnp.bfloat16), b.astype(jnp.bfloat16), preferred_element_type=jnp.float32)

    full = owned[...]
    gram = lax.dot_general(full, full, (((1,), (1,)), ((), ())), preferred_element_type=jnp.float32)
    gram_out[...] = gram.astype(jnp.bfloat16)
    gram_copy = pltpu.make_async_remote_copy(
        gram_out, gram_in, gram_send, gram_recv,
        device_id=dev(*peer), device_id_type=pl.DeviceIdType.MESH,
    )
    gram_copy.start()
    gram_copy.wait_recv()
    gram = gram + gram_in[...].astype(jnp.float32)
    order = gram.shape[0]
    diagonal = lax.broadcasted_iota(jnp.int32, (order, order), 0) == lax.broadcasted_iota(
        jnp.int32, (order, order), 1
    )
    trace = jnp.sum(jnp.where(diagonal, gram, 0.0), keepdims=True)
    inverse = 1.0 / (jnp.sqrt(trace) + 1e-07)
    gram = (gram * inverse) * inverse
    poly = second_coef * gram + third_coef * dot(gram, gram)
    mix = poly
    for _ in range(ITERS - 1):
        turned = dot(poly, gram)
        gram = first_coef * first_coef * gram + 2 * first_coef * turned + dot(poly, turned)
        before = poly
        poly = second_coef * gram + third_coef * dot(gram, gram)
        mix = first_coef * (before + poly) + dot(poly, before)
    lead = first_coef ** ITERS
    mix = mix.astype(jnp.bfloat16)
    scale = inverse * (0.2 * math.sqrt(width))

    def back_copy(i, j):
        copy = pltpu.make_async_remote_copy(
            result.at[j, pl.ds(i * rows, rows), :],
            update_hbm.at[
                owner_m, :, pl.ds(pl.multiple_of(my_half * half + j * step_cols, step_cols), step_cols)
            ],
            back_send.at[i * steps + j],
            back_recv.at[(owner_m * 2 + my_half) * steps + j],
            device_id=dev(jnp.int32(i), owner_g), device_id_type=pl.DeviceIdType.MESH,
        )
        local = pltpu.make_async_copy(
            result.at[j, pl.ds(i * rows, rows), :],
            update_hbm.at[
                owner_m, :, pl.ds(pl.multiple_of(my_half * half + j * step_cols, step_cols), step_cols)
            ],
            own_sem.at[j],
        )
        return copy, local

    for j in range(steps):
        block = owned[:, j * step_cols:(j + 1) * step_cols]
        made = lead * block.astype(jnp.float32) + jnp.dot(mix, block, preferred_element_type=jnp.float32)
        result[j] = (scale * made).astype(jnp.bfloat16)
        for i in range(size):
            copy, local = back_copy(i, j)

            @pl.when(jnp.logical_not(here(i)))
            def _():
                copy.start()

            @pl.when(here(i))
            def _():
                local.start()

    for copy in fsdp_copies + grp_copies:
        copy.wait_send()
    gram_copy.wait_send()
    for m in range(matrices):
        for h in range(2):
            copy, mine = out_copy(m, h)
            raw, _ = raw_copy(m, h)

            @pl.when(jnp.logical_not(mine))
            def _():
                raw.wait_send()
                copy.wait_send()

    store_new.wait()
    for j in range(steps):
        for i in range(size):
            copy, local = back_copy(i, j)

            @pl.when(jnp.logical_not(here(i)))
            def _():
                copy.wait_send()

            @pl.when(here(i))
            def _():
                local.wait()

    for m in range(matrices):
        for h in range(2):
            a, b = target(m, h)
            for j in range(steps):
                arrive = pltpu.make_async_remote_copy(
                    result.at[j, pl.ds(0, rows), :],
                    update_hbm.at[m, :, pl.ds(h * half + j * step_cols, step_cols)],
                    back_send.at[0], back_recv.at[(m * 2 + h) * steps + j],
                    device_id=dev(a, b), device_id_type=pl.DeviceIdType.MESH,
                )

                @pl.when(jnp.logical_not(jnp.logical_and(a == f, b == g)))
                def _():
                    arrive.wait_recv()


def load_rows(rows):
    return 32 if rows % 32 == 0 else rows


def store(update, new, update_hbm, new_hbm, sems):
    copies = [
        pltpu.make_async_copy(source.at[m], kept.at[m], sems.at[k, m])
        for k, (source, kept) in enumerate(((update, update_hbm), (new, new_hbm)))
        for m in range(update.shape[0])
    ]
    for copy in copies:
        copy.start()
    for copy in copies:
        copy.wait()


def local(groups, size, paired, grads, momentum, row_counts):
    matrices, rows, width = grads.shape
    half = width // 2
    step_cols = math.gcd(half, SEND_COLS)
    steps = half // step_cols
    order = size * rows
    dma = pltpu.SemaphoreType.DMA
    grads, momentum, row_counts = (
        pltpu.with_memory_space_constraint(value, pltpu.HBM) for value in (grads, momentum, row_counts)
    )
    update, new_momentum = pl.pallas_call(
        functools.partial(kernel, groups, size, paired),
        out_shape=(
            jax.ShapeDtypeStruct(grads.shape, jnp.bfloat16),
            jax.ShapeDtypeStruct(grads.shape, jnp.bfloat16),
        ),
        in_specs=[
            pl.BlockSpec(memory_space=pltpu.HBM),
            pl.BlockSpec(memory_space=pltpu.HBM),
            pl.BlockSpec(memory_space=pltpu.HBM),
        ],
        out_specs=(pl.BlockSpec(memory_space=pl.ANY), pl.BlockSpec(memory_space=pl.ANY)),
        scratch_shapes=[
            pltpu.SMEM(row_counts.shape, jnp.int32),
            pltpu.VMEM(grads.shape, jnp.bfloat16),
            pltpu.VMEM(grads.shape, jnp.bfloat16),
            pltpu.VMEM(grads.shape, jnp.bfloat16),
            pltpu.VMEM((order, half), jnp.bfloat16),
            pltpu.VMEM((matrices, 2, 2, rows, RAW_COLS), jnp.bfloat16),
            pltpu.VMEM((2, order, RAW_COLS), jnp.bfloat16),
            pltpu.VMEM((order, order), jnp.bfloat16),
            pltpu.VMEM((order, order), jnp.bfloat16),
            pltpu.VMEM((steps, order, step_cols), jnp.bfloat16),
            pltpu.VMEM((size, 16, 128), jnp.float32),
            pltpu.VMEM((groups, 16, 128), jnp.float32),
            dma,
            dma((2, matrices * (rows // load_rows(rows)))),
            dma,
            dma((steps,)),
            dma((size,)),
            dma((size,)),
            dma((groups,)),
            dma((groups,)),
            dma((2 * matrices,)),
            dma((size,)),
            dma((2 * matrices,)),
            dma((size,)),
            dma,
            dma,
            dma((size * steps,)),
            dma((2 * matrices * steps,)),
        ],
        compiler_params=pltpu.CompilerParams(
            collective_id=0, has_side_effects=True, vmem_limit_bytes=VMEM_BYTES
        ),
        cost_estimate=pl.CostEstimate(
            flops=4 * order * order * half, bytes_accessed=8 * grads.size, transcendentals=0
        ),
    )(row_counts, grads, momentum)
    return pl.pallas_call(
        store,
        out_shape=(
            jax.ShapeDtypeStruct(grads.shape, jnp.bfloat16),
            jax.ShapeDtypeStruct(grads.shape, jnp.bfloat16),
        ),
        in_specs=[pl.BlockSpec(memory_space=pl.ANY)] * 2,
        out_specs=(pl.BlockSpec(memory_space=pltpu.HBM), pl.BlockSpec(memory_space=pltpu.HBM)),
        scratch_shapes=[dma((2, matrices))],
        compiler_params=pltpu.CompilerParams(vmem_limit_bytes=VMEM_BYTES),
    )(update, new_momentum)


def chips_pair_groups(mesh):
    names = list(mesh.axis_names)
    grid = mesh.devices
    if names != ["fsdp", "grp"] or grid.shape[1] % 2:
        return False
    return all(
        getattr(grid[0, i], "coords", None) is not None
        and tuple(grid[0, i].coords) == tuple(grid[0, i + 1].coords)
        for i in range(0, grid.shape[1], 2)
    )


def solution(mesh):
    placed = (P("grp", "fsdp", None), P("grp", "fsdp", None), P("grp"))
    return jax.shard_map(
        functools.partial(local, mesh.shape["grp"], mesh.shape["fsdp"], chips_pair_groups(mesh)),
        mesh=mesh,
        in_specs=placed,
        out_specs=(P("grp", "fsdp", None), P("grp", "fsdp", None)),
        check_vma=False,
    )
```

```python
import functools
import math

import jax
import jax.numpy as jnp
from jax import lax
from jax.experimental import pallas as pl
from jax.experimental.pallas import tpu as pltpu
from jax.sharding import PartitionSpec as P

first_coef = 3.4445
second_coef = -4.775
third_coef = 2.0315

ROW_STEP = 16
SEND_COLS = 256
RAW_COLS = 128
VMEM_BYTES = 40 * 1024 * 1024


def kernel(
    groups, size, paired,
    counts_hbm, grads_hbm, momentum_hbm, update_hbm, new_hbm,
    counts_ref, grads, momentum, fresh, owned, raw_out, raw_in, gram_out, gram_in, result, fsdp_sums, grp_sums,
    count_sem, load_sem, store_sem, own_sem,
    fsdp_send, fsdp_recv, grp_send, grp_recv,
    raw_send, raw_recv, out_send, out_recv, gram_send, gram_recv, back_send, back_recv,
):
    matrices, rows, width = grads.shape
    half = width // 2
    step_cols = math.gcd(half, SEND_COLS)
    steps = half // step_cols
    f = lax.axis_index("fsdp")
    g = lax.axis_index("grp")

    def dev(a, b):
        return {"fsdp": a, "grp": b}

    if paired:
        core = lax.rem(g, 2)
        base = g - core
        owner_g = base + f // matrices
        owner_m = lax.rem(f, matrices)
        my_half = core
        peer = (f, base + 1 - core)

        def target(m, h):
            return core * matrices + m, base + h

        def nth(k):
            return jnp.where(core == 1, matrices - 1 - k, k)
    else:
        owner_g = g
        owner_m = f // 2
        my_half = lax.rem(f, 2)
        peer = (f + 1 - 2 * my_half, g)

        def target(m, h):
            return jnp.int32(2 * m + h), g

        def nth(k):
            return k

    barrier = pltpu.get_barrier_semaphore()
    others = [(lax.rem(f + d, size), g) for d in range(1, size)]
    others += [(f, lax.rem(g + d, groups)) for d in range(1, groups)]
    if paired:
        others += [(lax.rem(f + d, size), base + 1 - core) for d in range(1, size)]
    for a, b in others:
        pl.semaphore_signal(barrier, inc=1, device_id=dev(a, b), device_id_type=pl.DeviceIdType.MESH)

    load_counts = pltpu.make_async_copy(counts_hbm, counts_ref, count_sem)
    load_counts.start()
    piece = load_rows(rows)
    loads = [
        [
            pltpu.make_async_copy(
                source.at[m, pl.ds(r, piece), :], kept.at[m, pl.ds(r, piece), :],
                load_sem.at[k, m * (rows // piece) + r // piece],
            )
            for m in range(matrices)
            for r in range(0, rows, piece)
        ]
        for k, (source, kept) in enumerate(((grads_hbm, grads), (momentum_hbm, momentum)))
    ]
    for load in loads[0] + loads[1]:
        load.start()

    offset = f * rows

    def live_mask(m, r):
        ids = offset + r + lax.broadcasted_iota(jnp.int32, (ROW_STEP, 1), 0)
        return ids < counts_ref[m]

    load_counts.wait()
    acc = jnp.zeros((8, width), jnp.float32)
    for m in range(matrices):
        for r in range(0, rows, ROW_STEP):
            if r % piece == 0:
                loads[0][m * (rows // piece) + r // piece].wait()
            part = jnp.where(live_mask(m, r), grads[m, r:r + ROW_STEP, :].astype(jnp.float32), 0.0)
            part = part * part
            for k in range(0, ROW_STEP, 8):
                acc = acc + part[k:k + 8]
    tile = acc[:, :128]
    for k in range(128, width, 128):
        tile = tile + acc[:, k:k + 128]
    live_rows = jnp.int32(0)
    for m in range(matrices):
        live_rows = live_rows + jnp.clip(counts_ref[m] - offset, 0, rows)
    fsdp_sums[f, 0:8, :] = tile
    fsdp_sums[f, 8:16, :] = jnp.zeros((8, 128), jnp.float32) + live_rows.astype(jnp.float32)

    pl.semaphore_wait(barrier, len(others))

    def exchange(buf, me, count, place, send, recv):
        copies = []
        for d in range(1, count):
            a, b = place(lax.rem(me + d, count))
            copy = pltpu.make_async_remote_copy(
                buf.at[me], buf.at[me], send.at[d], recv.at[d],
                device_id=dev(a, b), device_id_type=pl.DeviceIdType.MESH,
            )
            copy.start()
            copies.append(copy)
        return copies

    def added(buf, copies):
        for copy in copies:
            copy.wait_recv()
        total = buf[0]
        for d in range(1, buf.shape[0]):
            total = total + buf[d]
        return total

    def raw_copy(m, h):
        a, b = target(m, h)
        copy = pltpu.make_async_remote_copy(
            raw_out.at[m, h],
            raw_in.at[:, pl.ds(pl.multiple_of(f * rows, 16), rows), :],
            raw_send.at[m * 2 + h], raw_recv.at[f],
            device_id=dev(a, b), device_id_type=pl.DeviceIdType.MESH,
        )
        return copy, jnp.logical_and(a == f, b == g)

    fsdp_copies = exchange(fsdp_sums, f, size, lambda i: (i, g), fsdp_send, fsdp_recv)
    for load in loads[1]:
        load.wait()
    for m in range(matrices):
        for h in range(2):
            for r in range(0, rows, ROW_STEP):
                live = live_mask(m, r)
                for k, kept in enumerate((grads, momentum)):
                    value = kept[m, r:r + ROW_STEP, h * half:h * half + RAW_COLS].astype(jnp.float32)
                    raw_out[m, h, k, r:r + ROW_STEP, :] = jnp.where(live, value, 0.0).astype(jnp.bfloat16)
            copy, mine = raw_copy(m, h)

            @pl.when(jnp.logical_not(mine))
            def _():
                copy.start()

    grp_sums[g] = added(fsdp_sums, fsdp_copies)
    grp_copies = exchange(grp_sums, g, groups, lambda i: (f, i), grp_send, grp_recv)
    total = added(grp_sums, grp_copies)
    square_sum = jnp.sum(total[0:8], keepdims=True)
    row_total = total[8:9, 0:1]
    clip = jnp.minimum(1.0, lax.rsqrt(square_sum / (row_total * width) + 1e-06))

    def out_copy(k, h):
        m = nth(k)
        a, b = target(m, h)
        copy = pltpu.make_async_remote_copy(
            fresh.at[m, :, pl.ds(h * half + RAW_COLS, half - RAW_COLS)],
            owned.at[pl.ds(pl.multiple_of(f * rows, 16), rows), pl.ds(RAW_COLS, half - RAW_COLS)],
            out_send.at[k * 2 + h], out_recv.at[f],
            device_id=dev(a, b), device_id_type=pl.DeviceIdType.MESH,
        )
        return copy, jnp.logical_and(a == f, b == g)

    for k in range(matrices):
        m = nth(k)
        for h in range(2):
            cols = slice(h * half, (h + 1) * half)
            for r in range(0, rows, ROW_STEP):
                at = (m, slice(r, r + ROW_STEP), cols)
                fresh[at] = jnp.where(
                    live_mask(m, r),
                    0.95 * momentum[at].astype(jnp.float32) + clip * grads[at].astype(jnp.float32),
                    0.0,
                ).astype(jnp.bfloat16)
            copy, mine = out_copy(k, h)

            @pl.when(jnp.logical_not(mine))
            def _():
                copy.start()

            @pl.when(mine)
            def _():
                owned[pl.ds(pl.multiple_of(f * rows, 16), rows), :] = fresh[m, :, cols]

    store_new = pltpu.make_async_copy(fresh, new_hbm, store_sem)
    store_new.start()

    def here(i):
        return jnp.logical_and(i == f, owner_g == g)

    for i in range(size):
        raw_arrive = pltpu.make_async_remote_copy(
            raw_out.at[0, 0], raw_in.at[:, pl.ds(i * rows, rows), :],
            raw_send.at[0], raw_recv.at[i],
            device_id=dev(f, owner_g), device_id_type=pl.DeviceIdType.MESH,
        )

        @pl.when(jnp.logical_not(here(i)))
        def _():
            raw_arrive.wait_recv()
            for r in range(i * rows, (i + 1) * rows, ROW_STEP):
                owned[r:r + ROW_STEP, 0:RAW_COLS] = (
                    0.95 * raw_in[1, r:r + ROW_STEP, :].astype(jnp.float32)
                    + clip * raw_in[0, r:r + ROW_STEP, :].astype(jnp.float32)
                ).astype(jnp.bfloat16)

    for i in range(size):
        arrive = pltpu.make_async_remote_copy(
            fresh.at[0, :, pl.ds(RAW_COLS, half - RAW_COLS)],
            owned.at[pl.ds(i * rows, rows), pl.ds(RAW_COLS, half - RAW_COLS)],
            out_send.at[0], out_recv.at[i],
            device_id=dev(f, owner_g), device_id_type=pl.DeviceIdType.MESH,
        )

        @pl.when(jnp.logical_not(here(i)))
        def _():
            arrive.wait_recv()

    def dot(a, b):
        return jnp.dot(a.astype(jnp.bfloat16), b.astype(jnp.bfloat16), preferred_element_type=jnp.float32)

    full = owned[...]
    gram = lax.dot_general(full, full, (((1,), (1,)), ((), ())), preferred_element_type=jnp.float32)
    gram_out[...] = gram.astype(jnp.bfloat16)
    gram_copy = pltpu.make_async_remote_copy(
        gram_out, gram_in, gram_send, gram_recv,
        device_id=dev(*peer), device_id_type=pl.DeviceIdType.MESH,
    )
    gram_copy.start()
    gram_copy.wait_recv()
    gram = gram + gram_in[...].astype(jnp.float32)
    order = gram.shape[0]
    diagonal = lax.broadcasted_iota(jnp.int32, (order, order), 0) == lax.broadcasted_iota(
        jnp.int32, (order, order), 1
    )
    trace = jnp.sum(jnp.where(diagonal, gram, 0.0), keepdims=True)
    inverse = 1.0 / (jnp.sqrt(trace) + 1e-07)
    gram = (gram * inverse) * inverse
    poly = second_coef * gram + third_coef * dot(gram, gram)
    both = dot(poly, jnp.concatenate([gram.astype(jnp.bfloat16), poly.astype(jnp.bfloat16)], axis=1))
    turned = first_coef * gram + both[:, :order]
    rest = 2 * first_coef * poly + both[:, order:]
    both = dot(turned, jnp.concatenate([poly.astype(jnp.bfloat16), rest.astype(jnp.bfloat16)], axis=1))
    after = first_coef * turned + both[:, :order]
    carried = first_coef * first_coef * turned + both[:, order:]
    mix = first_coef * poly + second_coef * carried + third_coef * dot(after, carried)
    lead = first_coef * first_coef
    mix = mix.astype(jnp.bfloat16)
    scale = inverse * (0.2 * math.sqrt(width))

    def back_to(d):
        return jnp.where(f < size // 2, size - 1 - d, d)

    def back_copy(d, j):
        i = back_to(d)
        copy = pltpu.make_async_remote_copy(
            result.at[j, pl.ds(pl.multiple_of(i * rows, 16), rows), :],
            update_hbm.at[
                owner_m, :, pl.ds(pl.multiple_of(my_half * half + j * step_cols, step_cols), step_cols)
            ],
            back_send.at[d * steps + j],
            back_recv.at[(owner_m * 2 + my_half) * steps + j],
            device_id=dev(i, owner_g), device_id_type=pl.DeviceIdType.MESH,
        )
        local = pltpu.make_async_copy(
            result.at[j, pl.ds(pl.multiple_of(i * rows, 16), rows), :],
            update_hbm.at[
                owner_m, :, pl.ds(pl.multiple_of(my_half * half + j * step_cols, step_cols), step_cols)
            ],
            own_sem.at[j],
        )
        return copy, local

    for j in range(steps):
        block = owned[:, j * step_cols:(j + 1) * step_cols]
        made = lead * block.astype(jnp.float32) + jnp.dot(mix, block, preferred_element_type=jnp.float32)
        result[j] = (scale * made).astype(jnp.bfloat16)
        for d in range(size):
            copy, local = back_copy(d, j)

            @pl.when(jnp.logical_not(here(back_to(d))))
            def _():
                copy.start()

            @pl.when(here(back_to(d)))
            def _():
                local.start()

    for copy in fsdp_copies + grp_copies:
        copy.wait_send()
    gram_copy.wait_send()
    for k in range(matrices):
        for h in range(2):
            copy, mine = out_copy(k, h)
            raw, raw_mine = raw_copy(k, h)

            @pl.when(jnp.logical_not(raw_mine))
            def _():
                raw.wait_send()

            @pl.when(jnp.logical_not(mine))
            def _():
                copy.wait_send()

    store_new.wait()
    for j in range(steps):
        for d in range(size):
            copy, local = back_copy(d, j)

            @pl.when(jnp.logical_not(here(back_to(d))))
            def _():
                copy.wait_send()

            @pl.when(here(back_to(d)))
            def _():
                local.wait()

    for m in range(matrices):
        for h in range(2):
            a, b = target(m, h)
            for j in range(steps):
                arrive = pltpu.make_async_remote_copy(
                    result.at[j, pl.ds(0, rows), :],
                    update_hbm.at[m, :, pl.ds(h * half + j * step_cols, step_cols)],
                    back_send.at[0], back_recv.at[(m * 2 + h) * steps + j],
                    device_id=dev(a, b), device_id_type=pl.DeviceIdType.MESH,
                )

                @pl.when(jnp.logical_not(jnp.logical_and(a == f, b == g)))
                def _():
                    arrive.wait_recv()


def load_rows(rows):
    return 32 if rows % 32 == 0 else rows


def store(update, new, update_hbm, new_hbm, sems):
    copies = [
        pltpu.make_async_copy(source.at[m], kept.at[m], sems.at[k, m])
        for k, (source, kept) in enumerate(((update, update_hbm), (new, new_hbm)))
        for m in range(update.shape[0])
    ]
    for copy in copies:
        copy.start()
    for copy in copies:
        copy.wait()


def local(groups, size, paired, grads, momentum, row_counts):
    matrices, rows, width = grads.shape
    half = width // 2
    step_cols = math.gcd(half, SEND_COLS)
    steps = half // step_cols
    order = size * rows
    dma = pltpu.SemaphoreType.DMA
    grads, momentum, row_counts = (
        pltpu.with_memory_space_constraint(value, pltpu.HBM) for value in (grads, momentum, row_counts)
    )
    update, new_momentum = pl.pallas_call(
        functools.partial(kernel, groups, size, paired),
        out_shape=(
            jax.ShapeDtypeStruct(grads.shape, jnp.bfloat16),
            jax.ShapeDtypeStruct(grads.shape, jnp.bfloat16),
        ),
        in_specs=[
            pl.BlockSpec(memory_space=pltpu.HBM),
            pl.BlockSpec(memory_space=pltpu.HBM),
            pl.BlockSpec(memory_space=pltpu.HBM),
        ],
        out_specs=(pl.BlockSpec(memory_space=pl.ANY), pl.BlockSpec(memory_space=pl.ANY)),
        scratch_shapes=[
            pltpu.SMEM(row_counts.shape, jnp.int32),
            pltpu.VMEM(grads.shape, jnp.bfloat16),
            pltpu.VMEM(grads.shape, jnp.bfloat16),
            pltpu.VMEM(grads.shape, jnp.bfloat16),
            pltpu.VMEM((order, half), jnp.bfloat16),
            pltpu.VMEM((matrices, 2, 2, rows, RAW_COLS), jnp.bfloat16),
            pltpu.VMEM((2, order, RAW_COLS), jnp.bfloat16),
            pltpu.VMEM((order, order), jnp.bfloat16),
            pltpu.VMEM((order, order), jnp.bfloat16),
            pltpu.VMEM((steps, order, step_cols), jnp.bfloat16),
            pltpu.VMEM((size, 16, 128), jnp.float32),
            pltpu.VMEM((groups, 16, 128), jnp.float32),
            dma,
            dma((2, matrices * (rows // load_rows(rows)))),
            dma,
            dma((steps,)),
            dma((size,)),
            dma((size,)),
            dma((groups,)),
            dma((groups,)),
            dma((2 * matrices,)),
            dma((size,)),
            dma((2 * matrices,)),
            dma((size,)),
            dma,
            dma,
            dma((size * steps,)),
            dma((2 * matrices * steps,)),
        ],
        compiler_params=pltpu.CompilerParams(
            collective_id=0, has_side_effects=True, vmem_limit_bytes=VMEM_BYTES
        ),
        cost_estimate=pl.CostEstimate(
            flops=4 * order * order * half, bytes_accessed=8 * grads.size, transcendentals=0
        ),
    )(row_counts, grads, momentum)
    return pl.pallas_call(
        store,
        out_shape=(
            jax.ShapeDtypeStruct(grads.shape, jnp.bfloat16),
            jax.ShapeDtypeStruct(grads.shape, jnp.bfloat16),
        ),
        in_specs=[pl.BlockSpec(memory_space=pl.ANY)] * 2,
        out_specs=(pl.BlockSpec(memory_space=pltpu.HBM), pl.BlockSpec(memory_space=pltpu.HBM)),
        scratch_shapes=[dma((2, matrices))],
        compiler_params=pltpu.CompilerParams(vmem_limit_bytes=VMEM_BYTES),
    )(update, new_momentum)


def chips_pair_groups(mesh):
    names = list(mesh.axis_names)
    grid = mesh.devices
    if names != ["fsdp", "grp"] or grid.shape[1] % 2:
        return False
    return all(
        getattr(grid[0, i], "coords", None) is not None
        and tuple(grid[0, i].coords) == tuple(grid[0, i + 1].coords)
        for i in range(0, grid.shape[1], 2)
    )


def solution(mesh):
    placed = (P("grp", "fsdp", None), P("grp", "fsdp", None), P("grp"))
    return jax.shard_map(
        functools.partial(local, mesh.shape["grp"], mesh.shape["fsdp"], chips_pair_groups(mesh)),
        mesh=mesh,
        in_specs=placed,
        out_specs=(P("grp", "fsdp", None), P("grp", "fsdp", None)),
        check_vma=False,
    )
```

```python
import functools
import math

import jax
import jax.numpy as jnp
from jax import lax
from jax.experimental import pallas as pl
from jax.experimental.pallas import tpu as pltpu
from jax.sharding import PartitionSpec as P

first_coef = 3.4445
second_coef = -4.775
third_coef = 2.0315

ROW_STEP = 16
SEND_COLS = 256
RAW_COLS = 128
GRAM_COLS = 256
VMEM_BYTES = 40 * 1024 * 1024


def kernel(
    groups, size, paired,
    counts_hbm, grads_hbm, momentum_hbm, update_hbm, new_hbm,
    counts_ref, grads, momentum, fresh, owned, raw_out, raw_in, gram_out, gram_in, result, fsdp_sums, grp_sums,
    count_sem, load_sem, store_sem, own_sem,
    fsdp_send, fsdp_recv, grp_send, grp_recv,
    raw_send, raw_recv, out_send, out_recv, gram_send, gram_recv, back_send, back_recv,
):
    matrices, rows, width = grads.shape
    half = width // 2
    step_cols = math.gcd(half, SEND_COLS)
    steps = half // step_cols
    f = lax.axis_index("fsdp")
    g = lax.axis_index("grp")

    def dev(a, b):
        return {"fsdp": a, "grp": b}

    if paired:
        core = lax.rem(g, 2)
        base = g - core
        owner_g = base + f // matrices
        owner_m = lax.rem(f, matrices)
        my_half = core
        peer = (f, base + 1 - core)

        def target(m, h):
            return core * matrices + m, base + h
    else:
        owner_g = g
        owner_m = f // 2
        my_half = lax.rem(f, 2)
        peer = (f + 1 - 2 * my_half, g)

        def target(m, h):
            return jnp.int32(2 * m + h), g

    barrier = pltpu.get_barrier_semaphore()
    others = [(lax.rem(f + d, size), g) for d in range(1, size)]
    others += [(f, lax.rem(g + d, groups)) for d in range(1, groups)]
    if paired:
        others += [(lax.rem(f + d, size), base + 1 - core) for d in range(1, size)]
    load_counts = pltpu.make_async_copy(counts_hbm, counts_ref, count_sem)
    load_counts.start()
    piece = load_rows(rows)
    loads = [
        [
            pltpu.make_async_copy(
                source.at[m, pl.ds(r, piece), :], kept.at[m, pl.ds(r, piece), :],
                load_sem.at[k, m * (rows // piece) + r // piece],
            )
            for m in range(matrices)
            for r in range(0, rows, piece)
        ]
        for k, (source, kept) in enumerate(((grads_hbm, grads), (momentum_hbm, momentum)))
    ]
    for load in loads[0]:
        load.start()
    for a, b in others:
        pl.semaphore_signal(barrier, inc=1, device_id=dev(a, b), device_id_type=pl.DeviceIdType.MESH)

    for load in loads[1]:
        load.start()

    offset = f * rows

    def live_mask(m, r):
        ids = offset + r + lax.broadcasted_iota(jnp.int32, (ROW_STEP, 1), 0)
        return ids < counts_ref[m]

    load_counts.wait()
    acc = jnp.zeros((8, width), jnp.float32)
    for m in range(matrices):
        for r in range(0, rows, ROW_STEP):
            if r % piece == 0:
                loads[0][m * (rows // piece) + r // piece].wait()
            part = jnp.where(live_mask(m, r), grads[m, r:r + ROW_STEP, :].astype(jnp.float32), 0.0)
            part = part * part
            for k in range(0, ROW_STEP, 8):
                acc = acc + part[k:k + 8]
    tile = acc[:, :128]
    for k in range(128, width, 128):
        tile = tile + acc[:, k:k + 128]
    live_rows = jnp.int32(0)
    for m in range(matrices):
        live_rows = live_rows + jnp.clip(counts_ref[m] - offset, 0, rows)
    fsdp_sums[f, 0:8, :] = tile
    fsdp_sums[f, 8:16, :] = jnp.zeros((8, 128), jnp.float32) + live_rows.astype(jnp.float32)

    pl.semaphore_wait(barrier, len(others))

    def exchange(buf, me, count, place, send, recv):
        copies = []
        for d in range(1, count):
            a, b = place(lax.rem(me + d, count))
            copy = pltpu.make_async_remote_copy(
                buf.at[me], buf.at[me], send.at[d], recv.at[d],
                device_id=dev(a, b), device_id_type=pl.DeviceIdType.MESH,
            )
            copy.start()
            copies.append(copy)
        return copies

    def added(buf, copies):
        for copy in copies:
            copy.wait_recv()
        total = buf[0]
        for d in range(1, buf.shape[0]):
            total = total + buf[d]
        return total

    def raw_copy(m, h):
        a, b = target(m, h)
        copy = pltpu.make_async_remote_copy(
            raw_out.at[m, h],
            raw_in.at[:, pl.ds(pl.multiple_of(f * rows, 16), rows), :],
            raw_send.at[m * 2 + h], raw_recv.at[f],
            device_id=dev(a, b), device_id_type=pl.DeviceIdType.MESH,
        )
        return copy, jnp.logical_and(a == f, b == g)

    fsdp_copies = exchange(fsdp_sums, f, size, lambda i: (i, g), fsdp_send, fsdp_recv)
    for load in loads[1]:
        load.wait()
    for m in range(matrices):
        for h in range(2):
            for r in range(0, rows, ROW_STEP):
                live = live_mask(m, r)
                for k, kept in enumerate((grads, momentum)):
                    value = kept[m, r:r + ROW_STEP, h * half:h * half + RAW_COLS].astype(jnp.float32)
                    raw_out[m, h, k, r:r + ROW_STEP, :] = jnp.where(live, value, 0.0).astype(jnp.bfloat16)
            copy, mine = raw_copy(m, h)

            @pl.when(jnp.logical_not(mine))
            def _():
                copy.start()

    grp_sums[g] = added(fsdp_sums, fsdp_copies)
    grp_copies = exchange(grp_sums, g, groups, lambda i: (f, i), grp_send, grp_recv)
    total = added(grp_sums, grp_copies)
    square_sum = jnp.sum(total[0:8], keepdims=True)
    row_total = total[8:9, 0:1]
    clip = jnp.minimum(1.0, lax.rsqrt(square_sum / (row_total * width) + 1e-06))

    def out_copy(m, h):
        a, b = target(m, h)
        copy = pltpu.make_async_remote_copy(
            fresh.at[m, :, pl.ds(h * half + RAW_COLS, half - RAW_COLS)],
            owned.at[pl.ds(pl.multiple_of(f * rows, 16), rows), pl.ds(RAW_COLS, half - RAW_COLS)],
            out_send.at[m * 2 + h], out_recv.at[f],
            device_id=dev(a, b), device_id_type=pl.DeviceIdType.MESH,
        )
        return copy, jnp.logical_and(a == f, b == g)

    for m in range(matrices):
        for h in range(2):
            cols = slice(h * half, (h + 1) * half)
            for r in range(0, rows, ROW_STEP):
                at = (m, slice(r, r + ROW_STEP), cols)
                fresh[at] = jnp.where(
                    live_mask(m, r),
                    0.95 * momentum[at].astype(jnp.float32) + clip * grads[at].astype(jnp.float32),
                    0.0,
                ).astype(jnp.bfloat16)
            copy, mine = out_copy(m, h)

            @pl.when(jnp.logical_not(mine))
            def _():
                copy.start()

            @pl.when(mine)
            def _():
                owned[pl.ds(pl.multiple_of(f * rows, 16), rows), :] = fresh[m, :, cols]

    store_new = pltpu.make_async_copy(fresh, new_hbm, store_sem)
    store_new.start()

    def here(i):
        return jnp.logical_and(i == f, owner_g == g)

    for i in range(size):
        raw_arrive = pltpu.make_async_remote_copy(
            raw_out.at[0, 0], raw_in.at[:, pl.ds(i * rows, rows), :],
            raw_send.at[0], raw_recv.at[i],
            device_id=dev(f, owner_g), device_id_type=pl.DeviceIdType.MESH,
        )

        @pl.when(jnp.logical_not(here(i)))
        def _():
            raw_arrive.wait_recv()
            for r in range(i * rows, (i + 1) * rows, ROW_STEP):
                owned[r:r + ROW_STEP, 0:RAW_COLS] = (
                    0.95 * raw_in[1, r:r + ROW_STEP, :].astype(jnp.float32)
                    + clip * raw_in[0, r:r + ROW_STEP, :].astype(jnp.float32)
                ).astype(jnp.bfloat16)

    for i in range(size):
        arrive = pltpu.make_async_remote_copy(
            fresh.at[0, :, pl.ds(RAW_COLS, half - RAW_COLS)],
            owned.at[pl.ds(i * rows, rows), pl.ds(RAW_COLS, half - RAW_COLS)],
            out_send.at[0], out_recv.at[i],
            device_id=dev(f, owner_g), device_id_type=pl.DeviceIdType.MESH,
        )

        @pl.when(jnp.logical_not(here(i)))
        def _():
            arrive.wait_recv()

    def dot(a, b):
        return jnp.dot(a.astype(jnp.bfloat16), b.astype(jnp.bfloat16), preferred_element_type=jnp.float32)

    full = owned[...]
    slabs = []
    for at, c in enumerate(range(0, full.shape[0], GRAM_COLS)):
        cols = slice(c, min(c + GRAM_COLS, full.shape[0]))
        part = lax.dot_general(
            full, owned[cols, :], (((1,), (1,)), ((), ())), preferred_element_type=jnp.float32
        )
        gram_out[:, cols] = part.astype(jnp.bfloat16)
        copy = pltpu.make_async_remote_copy(
            gram_out.at[:, pl.ds(c, cols.stop - c)], gram_in.at[:, pl.ds(c, cols.stop - c)],
            gram_send.at[at], gram_recv.at[at],
            device_id=dev(*peer), device_id_type=pl.DeviceIdType.MESH,
        )
        copy.start()
        slabs.append((copy, cols, part))
    parts = []
    for copy, cols, part in slabs:
        copy.wait_recv()
        parts.append(part + gram_in[:, cols].astype(jnp.float32))
    gram = jnp.concatenate(parts, axis=1)
    order = gram.shape[0]
    diagonal = lax.broadcasted_iota(jnp.int32, (order, order), 0) == lax.broadcasted_iota(
        jnp.int32, (order, order), 1
    )
    trace = jnp.sum(jnp.where(diagonal, gram, 0.0), keepdims=True)
    inverse = 1.0 / (jnp.sqrt(trace) + 1e-07)
    gram = (gram * inverse) * inverse
    poly = second_coef * gram + third_coef * dot(gram, gram)
    both = dot(poly, jnp.concatenate([gram.astype(jnp.bfloat16), poly.astype(jnp.bfloat16)], axis=1))
    turned = first_coef * gram + both[:, :order]
    rest = 2 * first_coef * poly + both[:, order:]
    both = dot(turned, jnp.concatenate([poly.astype(jnp.bfloat16), rest.astype(jnp.bfloat16)], axis=1))
    after = first_coef * turned + both[:, :order]
    carried = first_coef * first_coef * turned + both[:, order:]
    mix = first_coef * poly + second_coef * carried + third_coef * dot(after, carried)
    lead = first_coef * first_coef
    mix = mix.astype(jnp.bfloat16)
    scale = inverse * (0.2 * math.sqrt(width))

    def back_to(d):
        return jnp.where(f < size // 2, size - 1 - d, d)

    def back_copy(d, j):
        i = back_to(d)
        copy = pltpu.make_async_remote_copy(
            result.at[j, pl.ds(pl.multiple_of(i * rows, 16), rows), :],
            update_hbm.at[
                owner_m, :, pl.ds(pl.multiple_of(my_half * half + j * step_cols, step_cols), step_cols)
            ],
            back_send.at[d * steps + j],
            back_recv.at[(owner_m * 2 + my_half) * steps + j],
            device_id=dev(i, owner_g), device_id_type=pl.DeviceIdType.MESH,
        )
        local = pltpu.make_async_copy(
            result.at[j, pl.ds(pl.multiple_of(i * rows, 16), rows), :],
            update_hbm.at[
                owner_m, :, pl.ds(pl.multiple_of(my_half * half + j * step_cols, step_cols), step_cols)
            ],
            own_sem.at[j],
        )
        return copy, local

    for j in range(steps):
        block = owned[:, j * step_cols:(j + 1) * step_cols]
        made = lead * block.astype(jnp.float32) + jnp.dot(mix, block, preferred_element_type=jnp.float32)
        result[j] = (scale * made).astype(jnp.bfloat16)
        for d in range(size):
            copy, local = back_copy(d, j)

            @pl.when(jnp.logical_not(here(back_to(d))))
            def _():
                copy.start()

            @pl.when(here(back_to(d)))
            def _():
                local.start()

    for copy in fsdp_copies + grp_copies:
        copy.wait_send()
    for copy, _, _ in slabs:
        copy.wait_send()
    for m in range(matrices):
        for h in range(2):
            copy, mine = out_copy(m, h)
            raw, _ = raw_copy(m, h)

            @pl.when(jnp.logical_not(mine))
            def _():
                raw.wait_send()
                copy.wait_send()

    store_new.wait()
    for j in range(steps):
        for d in range(size):
            copy, local = back_copy(d, j)

            @pl.when(jnp.logical_not(here(back_to(d))))
            def _():
                copy.wait_send()

            @pl.when(here(back_to(d)))
            def _():
                local.wait()

    for m in range(matrices):
        for h in range(2):
            a, b = target(m, h)
            for j in range(steps):
                arrive = pltpu.make_async_remote_copy(
                    result.at[j, pl.ds(0, rows), :],
                    update_hbm.at[m, :, pl.ds(h * half + j * step_cols, step_cols)],
                    back_send.at[0], back_recv.at[(m * 2 + h) * steps + j],
                    device_id=dev(a, b), device_id_type=pl.DeviceIdType.MESH,
                )

                @pl.when(jnp.logical_not(jnp.logical_and(a == f, b == g)))
                def _():
                    arrive.wait_recv()


def load_rows(rows):
    return 32 if rows % 32 == 0 else rows


def store(update, new, update_hbm, new_hbm, sems):
    copies = [
        pltpu.make_async_copy(source.at[m], kept.at[m], sems.at[k, m])
        for k, (source, kept) in enumerate(((update, update_hbm), (new, new_hbm)))
        for m in range(update.shape[0])
    ]
    for copy in copies:
        copy.start()
    for copy in copies:
        copy.wait()


def local(groups, size, paired, grads, momentum, row_counts):
    matrices, rows, width = grads.shape
    half = width // 2
    step_cols = math.gcd(half, SEND_COLS)
    steps = half // step_cols
    order = size * rows
    dma = pltpu.SemaphoreType.DMA
    grads, momentum, row_counts = (
        pltpu.with_memory_space_constraint(value, pltpu.HBM) for value in (grads, momentum, row_counts)
    )
    update, new_momentum = pl.pallas_call(
        functools.partial(kernel, groups, size, paired),
        out_shape=(
            jax.ShapeDtypeStruct(grads.shape, jnp.bfloat16),
            jax.ShapeDtypeStruct(grads.shape, jnp.bfloat16),
        ),
        in_specs=[
            pl.BlockSpec(memory_space=pltpu.HBM),
            pl.BlockSpec(memory_space=pltpu.HBM),
            pl.BlockSpec(memory_space=pltpu.HBM),
        ],
        out_specs=(pl.BlockSpec(memory_space=pl.ANY), pl.BlockSpec(memory_space=pl.ANY)),
        scratch_shapes=[
            pltpu.SMEM(row_counts.shape, jnp.int32),
            pltpu.VMEM(grads.shape, jnp.bfloat16),
            pltpu.VMEM(grads.shape, jnp.bfloat16),
            pltpu.VMEM(grads.shape, jnp.bfloat16),
            pltpu.VMEM((order, half), jnp.bfloat16),
            pltpu.VMEM((matrices, 2, 2, rows, RAW_COLS), jnp.bfloat16),
            pltpu.VMEM((2, order, RAW_COLS), jnp.bfloat16),
            pltpu.VMEM((order, order), jnp.bfloat16),
            pltpu.VMEM((order, order), jnp.bfloat16),
            pltpu.VMEM((steps, order, step_cols), jnp.bfloat16),
            pltpu.VMEM((size, 16, 128), jnp.float32),
            pltpu.VMEM((groups, 16, 128), jnp.float32),
            dma,
            dma((2, matrices * (rows // load_rows(rows)))),
            dma,
            dma((steps,)),
            dma((size,)),
            dma((size,)),
            dma((groups,)),
            dma((groups,)),
            dma((2 * matrices,)),
            dma((size,)),
            dma((2 * matrices,)),
            dma((size,)),
            dma((-(-order // GRAM_COLS),)),
            dma((-(-order // GRAM_COLS),)),
            dma((size * steps,)),
            dma((2 * matrices * steps,)),
        ],
        compiler_params=pltpu.CompilerParams(
            collective_id=0, has_side_effects=True, vmem_limit_bytes=VMEM_BYTES
        ),
        cost_estimate=pl.CostEstimate(
            flops=4 * order * order * half, bytes_accessed=8 * grads.size, transcendentals=0
        ),
    )(row_counts, grads, momentum)
    return pl.pallas_call(
        store,
        out_shape=(
            jax.ShapeDtypeStruct(grads.shape, jnp.bfloat16),
            jax.ShapeDtypeStruct(grads.shape, jnp.bfloat16),
        ),
        in_specs=[pl.BlockSpec(memory_space=pl.ANY)] * 2,
        out_specs=(pl.BlockSpec(memory_space=pltpu.HBM), pl.BlockSpec(memory_space=pltpu.HBM)),
        scratch_shapes=[dma((2, matrices))],
        compiler_params=pltpu.CompilerParams(vmem_limit_bytes=VMEM_BYTES),
    )(update, new_momentum)


def chips_pair_groups(mesh):
    names = list(mesh.axis_names)
    grid = mesh.devices
    if names != ["fsdp", "grp"] or grid.shape[1] % 2:
        return False
    return all(
        getattr(grid[0, i], "coords", None) is not None
        and tuple(grid[0, i].coords) == tuple(grid[0, i + 1].coords)
        for i in range(0, grid.shape[1], 2)
    )


def solution(mesh):
    placed = (P("grp", "fsdp", None), P("grp", "fsdp", None), P("grp"))
    return jax.shard_map(
        functools.partial(local, mesh.shape["grp"], mesh.shape["fsdp"], chips_pair_groups(mesh)),
        mesh=mesh,
        in_specs=placed,
        out_specs=(P("grp", "fsdp", None), P("grp", "fsdp", None)),
        check_vma=False,
    )
```
